256 devices in a mesh: vel: 16 (over z_lo, x), gx: 8 (over y, core), gy: 2 (over z_hi).
Axes of the slice: x: 4, y: 4, z: 8 (z_hi: 2, z_lo: 4; z = z_hi * 4 + z_lo), core: 2. Of those that a mesh axis runs over, the one named last changes fastest.
Arguments:
- dist: float32 [3, 3, 128, 64, 4096], P(None, None, 'gx', 'gy', 'vel'), as said below
- cell_kind: int32 [128, 64], replicated, may hold values from 0 to 1, as said below
- inflow: float32 [4096], P('vel'), may hold values from 0.05 to 1.5
Outputs:
- dist_next: float32 [3, 3, 128, 64, 4096], P(None, None, 'gx', 'gy', 'vel')
- node_fields: float32 [5, 3, 3, 128, 64], P(None, None, None, 'gx', 'gy')
The draws below stay inside these ranges and needn't reach their ends.
Inputs may be any that keep to these rules, and one draw needn't show every extreme that they name: `dist`: every entry is positive. `cell_kind`: the ones form a single disc of elements that touches no edge of the grid.
All inputs are finite; a program needn't handle non-finite values.
Results may differ from the reference program's by a relative error of at most 0.00013.
Values sent between devices are 32-bit elements; how exact they have to be, the bound alone decides.
No kernel may reach another device: no remote copies, remote signals or barrier semaphores. Data moves between devices by JAX's collectives and lax.ppermute only.
A program may use at most 128 MiB of HBM per device.

```python
import math
import jax
import jax.numpy as jnp
from jax import lax

NV = 16
VELS = 4096
NX = 128
NY = 64


def draw_dist(key, part):
    key = jax.random.fold_in(key, 1)
    keys = jax.random.split(key, 5)
    spacing = 10.0 / NV
    index = jnp.arange(VELS, dtype=jnp.int32)

    def coordinate(level):
        return ((level.astype(jnp.float32) + 0.5) * spacing - 5.0)[None, None, None, None, :]
    speed_x = coordinate(index // (NV * NV))
    speed_y = coordinate(index // NV % NV)
    speed_z = coordinate(index % NV)
    cell_shape = (1, 1, NX, NY, 1)
    full_shape = (3, 3, NX, NY, VELS)
    particle_crowding = jnp.exp(jax.random.uniform(keys[0], cell_shape, jnp.float32, math.log(0.5), math.log(2.0)))
    drift = jax.random.uniform(keys[1], cell_shape, jnp.float32, -1.0, 1.5)
    heat = jnp.exp(jax.random.uniform(keys[2], cell_shape, jnp.float32, math.log(0.6), math.log(1.6)))
    rough = jnp.exp(jax.random.uniform(keys[3], full_shape, jnp.float32, -0.4, 0.4))
    cross = jax.random.uniform(keys[4], cell_shape, jnp.float32, -0.5, 0.5)
    heat_variance = (speed_x - drift) ** 2 + (speed_y - cross) ** 2 + speed_z ** 2
    return particle_crowding / (heat * jnp.sqrt(heat)) * jnp.exp(-heat_variance / (2.0 * heat)) * rough


def draw_cell_kind(key, part):
    key = jax.random.fold_in(key, 2)
    keys = jax.random.split(key, 3)
    least = min(NX, NY)
    radius = jax.random.randint(keys[0], (), least // 8, least // 4)
    centre_x = jax.random.randint(keys[1], (), NX // 4, 3 * NX // 4)
    centre_y = jax.random.randint(keys[2], (), NY // 4, 3 * NY // 4)
    column = jnp.arange(NX, dtype=jnp.int32)[:, None]
    row_pos = jnp.arange(NY, dtype=jnp.int32)[None, :]
    inside = (column - centre_x) ** 2 + (row_pos - centre_y) ** 2 <= radius * radius
    return inside.astype(jnp.int32)


def levels(rng, dims, pieces, low, high):
    level = 1.0
    for position, parts in pieces:
        draws = jax.random.uniform(jax.random.fold_in(jax.random.fold_in(rng, 6), position), (parts,), jnp.float32, low / len(pieces), high / len(pieces))
        level = level * jnp.repeat(jnp.exp(draws), dims[position] // parts).reshape((-1,) + (1,) * (len(dims) - 1 - position))
    return level


def setup_inputs(seed: int = 0) -> dict:
    key_list = jax.random.split(jax.random.key(seed), 4)
    dist = draw_dist(jax.random.fold_in(key_list[3], 71), 0)
    cell_kind = draw_cell_kind(jax.random.fold_in(key_list[3], 71), 0)
    inflow = jnp.clip(jnp.exp(math.log(1.5) - 3.4011974 * jax.random.uniform(key_list[2], (VELS,), jnp.float32) ** levels(key_list[2], (VELS,), ((0, 16),), -0.2, 0.2)), 0.05, 1.5)
    return dict(dist=dist, cell_kind=cell_kind, inflow=inflow)


vel_max = 5.0
rarefaction_ratio = 0.25
time_step = 0.08

def velocity_grid(index):
    spacing = 2.0 * vel_max / NV

    def coordinate(level):
        return (level.astype(jnp.float32) + 0.5) * spacing - vel_max
    return (coordinate(index // (NV * NV)), coordinate(index // NV % NV), coordinate(index % NV))

def quad_weight():
    spacing = 2.0 * vel_max / NV
    return spacing ** 3 / (2.0 * math.pi) ** 1.5

def moment_rows(index):
    speed_x, speed_y, speed_z = velocity_grid(index)
    weights = [jnp.ones_like(speed_x), speed_x, speed_y, speed_z, 0.5 * (speed_x * speed_x + speed_y * speed_y + speed_z * speed_z), jnp.maximum(-speed_x, 0.0), jnp.maximum(speed_x, 0.0), jnp.maximum(-speed_y, 0.0), jnp.maximum(speed_y, 0.0)]
    return quad_weight() * jnp.stack(weights)

def wall_scale():
    speed_x, speed_y, speed_z = velocity_grid(jnp.arange(NV * NV * NV, dtype=jnp.int32))
    energy = speed_x * speed_x + speed_y * speed_y + speed_z * speed_z
    return jnp.sum(quad_weight() * jnp.maximum(-speed_x, 0.0) * jnp.exp(-0.5 * energy))

def split_sums(totals):
    fluid_averages = totals[:5]
    exit_edge_condition = jnp.stack([totals[5][0], totals[6][2], totals[7][:, 0], totals[8][:, 2]])
    return (fluid_averages, exit_edge_condition)

def parameters(fluid_averages, exit_edge_condition, heat_speed_factor):
    particle_crowding = fluid_averages[0]
    mean_flow_first_axis = fluid_averages[1] / particle_crowding
    mean_flow_second_axis = fluid_averages[2] / particle_crowding
    mean_flow_third_axis = fluid_averages[3] / particle_crowding
    kinetic_heat_level = 2.0 / 3.0 * (fluid_averages[4] / particle_crowding - 0.5 * (mean_flow_first_axis * mean_flow_first_axis + mean_flow_second_axis * mean_flow_second_axis + mean_flow_third_axis * mean_flow_third_axis))
    return (jnp.stack([particle_crowding, mean_flow_first_axis, mean_flow_second_axis, mean_flow_third_axis, kinetic_heat_level]), exit_edge_condition / heat_speed_factor)

def derivative(field, axis):
    first = lax.index_in_dim(field, 0, axis)
    middle = lax.index_in_dim(field, 1, axis)
    final = lax.index_in_dim(field, 2, axis)
    return jnp.concatenate([-1.5 * first + 2.0 * middle - 0.5 * final, 0.5 * (final - first), 0.5 * first - 2.0 * middle + 1.5 * final], axis)

def neighbor_kinds(cell_kind, start_x, start_y, width_x, width_y):
    padded = jnp.pad(cell_kind, 1)

    def window(off_x, off_y):
        return lax.dynamic_slice(padded, (start_x + off_x, start_y + off_y), (width_x, width_y))[:, :, None]
    return (window(1, 1), window(0, 1), window(2, 1), window(1, 0), window(1, 2))

def edge_masks(start_x, start_y, width_x, width_y, total_x, total_y):
    column = start_x + jnp.arange(width_x, dtype=jnp.int32)
    row_pos = start_y + jnp.arange(width_y, dtype=jnp.int32)
    return ((column == 0)[:, None, None], (column == total_x - 1)[:, None, None], (row_pos == 0)[None, :, None], (row_pos == total_y - 1)[None, :, None])

def section(planes, index, inflow_part, node_fields, wall_density, kinds, edges, raw):
    speed_x, speed_y, speed_z = velocity_grid(index)
    energy = speed_x * speed_x + speed_y * speed_y + speed_z * speed_z
    wall_shape = jnp.exp(-0.5 * energy)
    own_kind, kind_left, kind_right, kind_below, kind_above = kinds
    first_col, last_col, first_row, last_row = edges
    left_raw, right_raw, below_raw, above_raw = raw
    left_side = jnp.where(first_col, inflow_part, jnp.where(kind_left == 1, wall_density[0][..., None] * wall_shape, left_raw))
    right_side = jnp.where(last_col, planes[2], jnp.where(kind_right == 1, wall_density[1][..., None] * wall_shape, right_raw))
    below_side = jnp.where(first_row, planes[:, 0], jnp.where(kind_below == 1, wall_density[2][..., None] * wall_shape, below_raw))
    above_side = jnp.where(last_row, planes[:, 2], jnp.where(kind_above == 1, wall_density[3][..., None] * wall_shape, above_raw))
    particle_crowding = node_fields[0][..., None]
    mean_flow_first_axis = node_fields[1][..., None]
    mean_flow_second_axis = node_fields[2][..., None]
    mean_flow_third_axis = node_fields[3][..., None]
    kinetic_heat_level = node_fields[4][..., None]
    heat_variance = (speed_x - mean_flow_first_axis) ** 2 + (speed_y - mean_flow_second_axis) ** 2 + (speed_z - mean_flow_third_axis) ** 2
    gaussian_target_state = particle_crowding / (kinetic_heat_level * jnp.sqrt(kinetic_heat_level)) * jnp.exp(-heat_variance / (2.0 * kinetic_heat_level))
    bgk_decay_update = particle_crowding * jnp.sqrt(kinetic_heat_level) / rarefaction_ratio
    update = -2.0 * (speed_x * derivative(planes, 0) + speed_y * derivative(planes, 1)) + bgk_decay_update * (gaussian_target_state - planes)
    update = update.at[0].add(6.0 * jnp.maximum(speed_x, 0.0) * (left_side - planes[0]))
    update = update.at[2].add(6.0 * jnp.maximum(-speed_x, 0.0) * (right_side - planes[2]))
    update = update.at[:, 0].add(6.0 * jnp.maximum(speed_y, 0.0) * (below_side - planes[:, 0]))
    update = update.at[:, 2].add(6.0 * jnp.maximum(-speed_y, 0.0) * (above_side - planes[:, 2]))
    return jnp.where(own_kind == 1, planes, planes + time_step * update)

def reference(dist, cell_kind, inflow):
    block = NV * NV

    def accumulate(level, total):
        start = (jnp.asarray(level).astype(jnp.int32) * block).astype(jnp.int32)
        index = start + jnp.arange(block, dtype=jnp.int32)
        part = lax.dynamic_slice_in_dim(dist, start, block, 4)
        product = jnp.dot(part.reshape(-1, block), moment_rows(index).T, precision=lax.Precision.HIGHEST, preferred_element_type=jnp.float32)
        return total + product
    totals = lax.fori_loop(0, NV, accumulate, jnp.zeros((9 * NX * NY, 9), jnp.float32))
    fluid_averages, exit_edge_condition = split_sums(totals.T.reshape(9, 3, 3, NX, NY))
    node_fields, wall_density = parameters(fluid_averages, exit_edge_condition, wall_scale())
    kinds = neighbor_kinds(cell_kind, 0, 0, NX, NY)
    edges = edge_masks(0, 0, NX, NY, NX, NY)

    def advance(level, result):
        start = (jnp.asarray(level).astype(jnp.int32) * block).astype(jnp.int32)
        index = start + jnp.arange(block, dtype=jnp.int32)
        part = lax.dynamic_slice_in_dim(dist, start, block, 4)
        inflow_part = lax.dynamic_slice_in_dim(inflow, start, block, 0)
        zero_x = jnp.zeros_like(part[0, :, :1])
        zero_y = jnp.zeros_like(part[:, 0, :, :1])
        left_raw = jnp.concatenate([zero_x, part[2, :, :-1]], 1)
        right_raw = jnp.concatenate([part[0, :, 1:], zero_x], 1)
        below_raw = jnp.concatenate([zero_y, part[:, 2, :, :-1]], 2)
        above_raw = jnp.concatenate([part[:, 0, :, 1:], zero_y], 2)
        fresh = section(part, index, inflow_part, node_fields, wall_density, kinds, edges, (left_raw, right_raw, below_raw, above_raw))
        return lax.dynamic_update_slice_in_dim(result, fresh, start, 4)
    dist_next = lax.fori_loop(0, NV, advance, jnp.zeros_like(dist))
    return (dist_next, node_fields)
```

```python
import math

import jax
import jax.numpy as jnp
import ml_dtypes
import numpy as np
from jax import lax
from jax.experimental import pallas as pl
from jax.experimental.pallas import tpu as pltpu
from jax.sharding import PartitionSpec as P

NV = 16
SPACING = 10.0 / NV
VEL_MAX = 5.0
RAREFACTION = 0.25
TIME_STEP = 0.08
WEIGHT = SPACING**3 / (2.0 * math.pi) ** 1.5

LANES = NV * NV
HALF = LANES // 2
SUM_ROWS = 208
TAIL = 160
COEF_ROWS = 32
MASK_ROWS = 16
CHUNKS = 4
F32 = jnp.float32
BF16 = jnp.bfloat16


def levels():
    return (np.arange(NV) + 0.5) * SPACING - VEL_MAX


def lane_speeds():
    return np.repeat(levels(), NV), np.tile(levels(), NV)


def wall_scale():
    level = levels()
    gauss = np.exp(-0.5 * level * level)
    return float(WEIGHT * np.sum(np.maximum(-level, 0.0) * gauss) * np.sum(gauss) ** 2)


def pieces(value, count):
    out = []
    for _ in range(count):
        piece = value.astype(ml_dtypes.bfloat16).astype(np.float64)
        out.append(piece)
        value = value - piece
    return out


def spread_weights():
    vy, vz = lane_speeds()
    square = vy * vy + vz * vz
    wall = np.exp(-0.5 * square)
    table = np.zeros((COEF_ROWS, 2 * LANES + HALF))
    high, low = pieces(square, 2)
    for row in range(3):
        table[row, :LANES] = 1.0
        table[3 + row, :LANES] = vy
        table[6 + row, :LANES] = vz
        table[9 + row, :LANES] = high
        table[12 + row, :LANES] = low
    table[15:17, 2 * LANES :] = 1.0
    for base, shape in (
        (17, wall),
        (20, np.maximum(vy, 0.0) * wall),
        (23, np.maximum(-vy, 0.0) * wall),
    ):
        first, second = pieces(shape, 2)
        table[base, LANES : 2 * LANES] = first
        table[base + 1, LANES : 2 * LANES] = second
        table[base + 2, LANES : 2 * LANES] = first
    return jnp.asarray(table.astype(ml_dtypes.bfloat16))


def own_speed():
    level = lax.axis_index("vel")
    return level, (level.astype(F32) + 0.5) * SPACING - VEL_MAX


def lane_axis(shape, axis):
    return lax.broadcasted_iota(jnp.int32, shape, axis)


def moment_weights():
    row = lane_axis((16, LANES), 0)
    lane = lane_axis((16, LANES), 1)
    vy = ((lane // NV).astype(F32) + 0.5) * SPACING - VEL_MAX
    vz = ((lane % NV).astype(F32) + 0.5) * SPACING - VEL_MAX
    square = vy * vy + vz * vz
    high = square.astype(BF16).astype(F32)
    table = jnp.zeros((16, LANES), F32)
    for at, value in enumerate(
        (1.0, vy, vz, high, square - high, jnp.maximum(-vy, 0.0), jnp.maximum(vy, 0.0))
    ):
        table = jnp.where(row == at, value, table)
    return table.astype(BF16)


def kind_masks(kinds, masks, wx, wy, forward):
    n = wx * wy
    size_y, size_x = kinds.shape
    start_x = lax.axis_index("gx") * wx
    start_y = lax.axis_index("gy") * wy
    behind = jnp.where(forward, 1, -1)
    kind = kinds[...].astype(F32).astype(BF16)
    x = lane_axis((size_x, n), 0)
    own_x = start_x + lane_axis((size_x, n), 1) // wy
    y = lane_axis((size_y, n), 0)
    own_y = start_y + lane_axis((size_y, n), 1) % wy

    def pick(column):
        chosen = jnp.where(x == column, 1.0, 0.0).astype(BF16)
        return jnp.dot(kind, chosen, preferred_element_type=F32)

    def at(table, row):
        return jnp.sum(jnp.where(y == row, table, 0.0), axis=0, keepdims=True)

    here = pick(own_x)
    fluid = 1.0 - at(here, own_y)
    solid_x = at(pick(own_x - behind), own_y)
    solid_b = at(here, own_y - 1)
    solid_a = at(here, own_y + 1)
    column, row = own_x[0:1], own_y[0:1]
    last_x = jnp.logical_and(jnp.logical_not(forward), column == size_x - 1)
    inner_x = jnp.where(last_x, 0.0, fluid)
    inner_b = jnp.where(row == 0, 0.0, fluid)
    inner_a = jnp.where(row == size_y - 1, 0.0, fluid)
    masks[...] = jnp.zeros_like(masks)
    for at_row, value in enumerate(
        (
            fluid,
            inner_x * (1.0 - solid_x),
            inner_x,
            inner_b * (1.0 - solid_b),
            inner_b,
            inner_a * (1.0 - solid_a),
            inner_a,
            fluid * solid_x,
            fluid * solid_b,
            fluid * solid_a,
        )
    ):
        masks[at_row : at_row + 1, :] = value


def moments_kernel(wx, wy, dist, kinds, sums, face_x, face_y, masks, dv, kind, sems):
    n = wx * wy
    copies = [pltpu.make_async_copy(dist.at[k], dv.at[k], sems.at[k]) for k in range(9)]
    kind_copy = pltpu.make_async_copy(kinds, kind, sems.at[9])
    copies[0].start()
    kind_copy.start()
    for copy in copies[1:]:
        copy.start()
    level, vx = own_speed()
    sums[...] = jnp.zeros_like(sums)
    table = moment_weights()
    kind_copy.wait()
    kind_masks(kind, masks, wx, wy, level >= NV // 2)
    forward = level >= NV // 2
    contract = (((1,), (1,)), ((), ()))

    def put(first, step, row):
        for c in range(n // HALF):
            at = first + c * step
            sums[at : at + 1, :] = row[:, c * HALF : (c + 1) * HALF]

    walls_x, walls_y = [None] * 3, [None] * 3
    for k in range(9):
        i, j = divmod(k, 3)
        copies[k].wait()
        plane = dv[k]
        high = plane.astype(BF16)
        low = (plane - high.astype(F32)).astype(BF16)
        part = lax.dot_general(table, high, contract, preferred_element_type=F32)
        part = part + lax.dot_general(table, low, contract, preferred_element_type=F32)
        part = part * WEIGHT
        total = part[0:1]
        rows = (
            total,
            vx * total,
            part[1:2],
            part[2:3],
            0.5 * (vx * vx * total + part[3:4] + part[4:5]),
        )
        for f, row in enumerate(rows):
            if k < 8:
                put(f * 32 + k, 8, row)
            else:
                put(TAIL + f * 4, 1, row)
        if i == 0:
            walls_x[j] = total
        if i == 2:
            put(TAIL + (5 + j) * 4, 1, jnp.abs(vx) * jnp.where(forward, total, walls_x[j]))
        if j == 0:
            walls_y[i] = part[5:6] * masks[8:9, :]
        if j == 2:
            put(TAIL + (8 + i) * 4, 1, walls_y[i] + part[6:7] * masks[9:10, :])

    @pl.when(level >= NV // 2)
    def _():
        for j in range(3):
            face_x[j] = dv[6 + j, n - wy : n, :]

    @pl.when(level < NV // 2)
    def _():
        for j in range(3):
            face_x[j] = dv[j, 0:wy, :]

    @pl.when(lax.axis_index("gy") == 0)
    def _():
        for i in range(3):
            for p in range(wx):
                at = p * wy + wy - 1
                face_y[i, p : p + 1, :] = dv[3 * i + 2, at : at + 1, HALF:]

    @pl.when(lax.axis_index("gy") != 0)
    def _():
        for i in range(3):
            for p in range(wx):
                at = p * wy
                face_y[i, p : p + 1, :] = dv[3 * i, at : at + 1, :HALF]


def advect_kernel(wx, wy, dist, table, masks, out, dv, edge_x, edge_y, weights, spread, sems):
    level, vx = own_speed()
    keep = pltpu.make_async_copy(table, weights, sems.at[CHUNKS])
    keep.start()
    row = lane_axis((MASK_ROWS, 7 * HALF), 0)
    column = lane_axis((MASK_ROWS, 7 * HALF), 1)
    select = jnp.where(column // HALF == row, 1.0, 0.0).astype(BF16)
    cx = -TIME_STEP * vx
    face_cx = 6.0 * TIME_STEP * jnp.abs(vx)
    lane = lane_axis((1, HALF), 1)
    q = lane_axis((wy, HALF), 0)

    def speed_y(half):
        return ((lane // NV + half * (NV // 2)).astype(F32) + 0.5) * SPACING - VEL_MAX

    def differences(a):
        four = 4.0 * a[1]
        rest = four - (a[0] + a[2])
        return rest - 2.0 * a[0], a[2] - a[0], 2.0 * a[2] - rest

    def tile(p, half, sign, trace):
        rows = pl.ds(pl.multiple_of(p * wy, wy), wy)
        lanes = slice(half * HALF, (half + 1) * HALF)
        vy = speed_y(half)
        cy = -TIME_STEP * vy
        face_cy = 6.0 * TIME_STEP * jnp.abs(vy)
        d = [[dv[3 * i + j, rows, lanes] for j in range(3)] for i in range(3)]
        fluid, wall_x, own_x, wall_b, own_b, wall_a, own_a = [
            spread[rows, m * HALF : (m + 1) * HALF] for m in range(7)
        ]
        dx = [differences([d[i][j] for i in range(3)]) for j in range(3)]
        for i in range(3):
            dy = differences(d[i])
            for j in range(3):
                value = d[i][j] + fluid * (cx * dx[j][i] + cy * dy[j])
                if i == (0 if sign > 0 else 2):
                    change = own_x * d[i][j]
                    if trace is not None:
                        change = change - wall_x * trace(j, lanes)
                    value = value - face_cx * change
                if half == 1 and j == 0:
                    raw = jnp.where(q == 0, 0.0, pltpu.roll(d[i][2], 1, 0))
                    value = value + face_cy * (wall_b * raw - own_b * d[i][j])
                if half == 0 and j == 2:
                    raw = jnp.where(q == wy - 1, 0.0, pltpu.roll(d[i][0], wy - 1, 0))
                    value = value + face_cy * (wall_a * raw - own_a * d[i][j])
                out[3 * i + j, rows, lanes] = value

    def sweep(sign):
        edge = 0 if sign > 0 else wx - 1
        source = 6 if sign > 0 else 0
        share = wx // CHUNKS
        order = range(CHUNKS) if sign > 0 else range(CHUNKS)[::-1]

        def part(chunk):
            rows = slice(chunk * share * wy, (chunk + 1) * share * wy)
            return pltpu.make_async_copy(dist.at[:, rows], dv.at[:, rows], sems.at[chunk])

        for chunk in order:
            part(chunk).start()
        spread[...] = lax.dot_general(
            masks[...].astype(BF16), select, (((0,), (0,)), ((), ())), preferred_element_type=F32
        )
        edge_x[...] = face_cx * spread[edge * wy : (edge + 1) * wy, HALF : 2 * HALF]
        for chunk in order:
            part(chunk).wait()
            low, high = chunk * share, (chunk + 1) * share
            if chunk == order[0]:
                for half in range(2):
                    tile(edge, half, sign, None)
                low, high = (low + 1, high) if sign > 0 else (low, high - 1)

            @pl.loop(low, high)
            def _(p):
                behind = pl.ds(pl.multiple_of((p - sign) * wy, wy), wy)
                for half in range(2):
                    tile(p, half, sign, lambda j, lanes: dv[source + j, behind, lanes])

    @pl.when(level >= NV // 2)
    def _():
        sweep(1)

    @pl.when(level < NV // 2)
    def _():
        sweep(-1)

    upper = lax.axis_index("gy") != 0

    @pl.when(upper)
    def _():
        for p in range(wx):
            at = p * wy
            edge_y[p : p + 1, :] = spread[at : at + 1, 3 * HALF : 4 * HALF] * (
                6.0 * TIME_STEP * speed_y(1)
            )

    @pl.when(jnp.logical_not(upper))
    def _():
        for p in range(wx):
            at = p * wy + wy - 1
            edge_y[p : p + 1, :] = spread[at : at + 1, 5 * HALF : 6 * HALF] * (
                -6.0 * TIME_STEP * speed_y(0)
            )

    keep.wait()


def edges_kernel(wx, wy, inside, halo_x, halo_y, inflow, edge_x, edge_y, out):
    del inside
    level, _ = own_speed()
    forward = level >= NV // 2
    upper = lax.axis_index("gy") != 0
    first_x = lax.axis_index("gx") == 0

    def along_x(p, i, outside):
        rows = slice(p * wy, (p + 1) * wy)
        for j in range(3):
            for half in range(2):
                lanes = slice(half * HALF, (half + 1) * HALF)
                out[3 * i + j, rows, lanes] += edge_x[...] * outside(j, lanes)

    def along_y(q, j, lanes):
        for i in range(3):
            for p in range(wx):
                at = slice(p * wy + q, p * wy + q + 1)
                out[3 * i + j, at, lanes] += edge_y[p : p + 1, :] * halo_y[i, p : p + 1, :]

    @pl.when(forward)
    def _():
        along_x(0, 0, lambda j, at: jnp.where(first_x, inflow[:, at], halo_x[j, :, at]))

    @pl.when(jnp.logical_not(forward))
    def _():
        along_x(wx - 1, 2, lambda j, at: halo_x[j, :, at])

    @pl.when(upper)
    def _():
        along_y(0, 0, slice(HALF, LANES))

    @pl.when(jnp.logical_not(upper))
    def _():
        along_y(wy - 1, 2, slice(0, HALF))


def split(value, count):
    out = []
    for _ in range(count):
        piece = value.astype(BF16).astype(F32)
        out.append(piece)
        value = value - piece
    return out


def relax_kernel(
    wx,
    wy,
    sums_a,
    sums_b,
    masks,
    table,
    advected,
    dv,
    out,
    fields_out,
    coef,
    fields,
    result,
    sems,
):
    n = wx * wy
    level, vx = own_speed()
    is_forward = level >= NV // 2
    parts = range(n // HALF)

    def wide(read, first, step, count):
        return jnp.concatenate(
            [read(slice(first + c * step, first + c * step + count)) for c in parts], axis=1
        )

    def both(rows):
        return sums_a[rows, :] + sums_b[rows, :]

    def received(rows):
        return sums_b[rows, :]

    fluid = masks[0:1, :]
    coef[...] = jnp.zeros_like(coef)
    log2e = math.log2(math.e)

    def store(planes, start, value, count):
        for piece_at, piece in enumerate(split(value, count)):
            coef[planes, start + piece_at, :] = piece

    for planes, where, s in (
        (slice(0, 8), 0, [wide(both, f * 32, 8, 8) for f in range(5)]),
        (slice(8, 9), 8, [wide(both, TAIL + f * 4, 1, 1) for f in range(5)]),
    ):
        rho = s[0]
        ux, uy, uz = s[1] / rho, s[2] / rho, s[3] / rho
        temp = 2.0 / 3.0 * (s[4] / rho - 0.5 * (ux * ux + uy * uy + uz * uz))
        for f, value in enumerate((rho, ux, uy, uz, temp)):
            at = f * 9 + where
            fields[at : at + value.shape[0], :] = value
        rate = rho * jnp.sqrt(temp) / RAREFACTION * TIME_STEP * fluid
        slope = (0.5 * log2e) / temp
        height = (
            2.0 * jnp.log2(rho)
            - jnp.log2(temp)
            + math.log2(TIME_STEP / RAREFACTION)
            - slope * ((vx - ux) * (vx - ux) + uy * uy + uz * uz)
        )
        height = jnp.where(fluid == 0.0, -1e30, height)
        store(planes, 0, height, 3)
        store(planes, 3, 2.0 * slope * uy, 3)
        store(planes, 6, 2.0 * slope * uz, 3)
        store(planes, 9, -slope, 3)
        store(planes, 12, -slope, 3)
        store(planes, 15, rate, 2)

    def store_wall(k, start, value):
        first, second = split(value, 2)
        coef[k, start : start + 1, :] = first
        coef[k, start + 1 : start + 2, :] = first
        coef[k, start + 2 : start + 3, :] = second

    scale = 6.0 * TIME_STEP / wall_scale()
    forward = is_forward.astype(F32)
    gauss_x = jnp.exp(jnp.full((1, n), -0.5, F32) * (vx * vx)) * scale
    solid_x = masks[7:8, :] * gauss_x * jnp.abs(vx)
    solid_b = masks[8:9, :] * gauss_x
    solid_a = masks[9:10, :] * gauss_x
    for j in range(3):
        value = solid_x * wide(received, TAIL + (5 + j) * 4, 1, 1)
        store_wall(j, 17, value * forward)
        store_wall(6 + j, 17, value * (1.0 - forward))
    for i in range(3):
        value = wide(both, TAIL + (8 + i) * 4, 1, 1)
        store_wall(3 * i, 20, solid_b * value)
        store_wall(3 * i + 2, 23, solid_a * value)

    weights = table[...]
    chunk = min(256, n)
    copies = []
    for k in range(9):
        for start in range(0, n, chunk):
            rows = slice(start, start + chunk)
            spread = lax.dot_general(
                coef[k, :, rows].astype(BF16),
                weights,
                (((0,), (0,)), ((), ())),
                preferred_element_type=F32,
            )
            rate = spread[:, 2 * LANES :]
            for half in range(2):
                lanes = slice(half * HALF, (half + 1) * HALF)
                target = jnp.exp2(spread[:, lanes])
                wall = spread[:, LANES + half * HALF : LANES + (half + 1) * HALF]
                result[k, rows, lanes] = (
                    advected[k, rows, lanes] - rate * dv[k, rows, lanes] + (target + wall)
                )
        copy = pltpu.make_async_copy(result.at[k], out.at[k], sems.at[k])
        copy.start()
        copies.append(copy)
    for p in range(wx):
        fields_out[:, p, :] = fields[0:45, p * wy : (p + 1) * wy]
    for copy in copies:
        copy.wait()


def exchanges():
    count = lax.axis_size("vel")
    return (
        [(v, v ^ 1) for v in range(count)],
        [(v, v ^ 3) for v in range(count)],
        [(v, v ^ 4) for v in range(count)],
        [(v, v ^ 8) for v in range(count)],
    )


def upwind_pairs():
    count = lax.axis_size("gx")
    pairs = []
    for v in range(lax.axis_size("vel")):
        step = 1 if v >= NV // 2 else -1
        for g in range(count):
            if 0 <= g + step < count:
                pairs.append((v * count + g, v * count + g + step))
    return pairs


def vmem(shape):
    return pltpu.VMEM(shape, F32)


def in_vmem(x):
    return pltpu.with_memory_space_constraint(x, pltpu.VMEM)


def shards(dist, cell_kind, inflow):
    wx, wy = dist.shape[2], dist.shape[3]
    n = wx * wy
    whole = pl.BlockSpec(memory_space=pltpu.VMEM)
    anywhere = pl.BlockSpec(memory_space=pl.ANY)
    planes = pltpu.with_memory_space_constraint(dist.reshape(9, n, LANES), pltpu.HBM)
    sums, face_x, face_y, masks = pl.pallas_call(
        lambda *refs: moments_kernel(wx, wy, *refs),
        out_shape=(
            vmem((SUM_ROWS, HALF)),
            vmem((3, wy, LANES)),
            vmem((3, wx, HALF)),
            vmem((MASK_ROWS, n)),
        ),
        in_specs=[anywhere, anywhere],
        out_specs=(whole, whole, whole, whole),
        scratch_shapes=[
            pltpu.VMEM((9, n, LANES), F32),
            pltpu.VMEM(cell_kind.shape[::-1], jnp.int32),
            pltpu.SemaphoreType.DMA((10,)),
        ],
        compiler_params=pltpu.CompilerParams(vmem_limit_bytes=16 << 20),
        cost_estimate=pl.CostEstimate(
            flops=2 * 32 * 9 * n * LANES, bytes_accessed=4 * 9 * n * LANES, transcendentals=0
        ),
        name="moments",
    )(planes, pltpu.with_memory_space_constraint(cell_kind.T, pltpu.HBM))
    table = spread_weights()
    advected, held, edge_x, edge_y, table = pl.pallas_call(
        lambda *refs: advect_kernel(wx, wy, *refs),
        out_shape=(
            vmem((9, n, LANES)),
            vmem((9, n, LANES)),
            vmem((wy, HALF)),
            vmem((wx, HALF)),
            pltpu.VMEM(table.shape, table.dtype),
        ),
        in_specs=[anywhere, anywhere, whole],
        out_specs=(whole,) * 5,
        scratch_shapes=[pltpu.VMEM((n, 7 * HALF), F32), pltpu.SemaphoreType.DMA((CHUNKS + 1,))],
        compiler_params=pltpu.CompilerParams(vmem_limit_bytes=8 << 20),
        cost_estimate=pl.CostEstimate(
            flops=20 * 9 * n * LANES, bytes_accessed=12 * 9 * n * LANES, transcendentals=0
        ),
        name="advect",
    )(planes, pltpu.with_memory_space_constraint(table, pltpu.HBM), masks)
    steps = exchanges()
    total = sums + lax.ppermute(sums, "vel", steps[0])
    total = total + lax.ppermute(total, "vel", steps[1])
    total, edge_x, edge_y = lax.optimization_barrier((total, edge_x, edge_y))
    halo_x = lax.ppermute(face_x, ("vel", "gx"), upwind_pairs())
    total = total + lax.ppermute(total, "vel", steps[2])
    total, halo_x = lax.optimization_barrier((total, halo_x))
    other = lax.ppermute(total, "vel", steps[3])
    halo_y = lax.ppermute(face_y, "gy", [(0, 1), (1, 0)])
    advected = pl.pallas_call(
        lambda *refs: edges_kernel(wx, wy, *refs),
        out_shape=vmem((9, n, LANES)),
        in_specs=[whole] * 6,
        out_specs=whole,
        input_output_aliases={0: 0},
        compiler_params=pltpu.CompilerParams(vmem_limit_bytes=4 << 20),
        cost_estimate=pl.CostEstimate(
            flops=100 * 9 * n * LANES, bytes_accessed=40 * 9 * n * LANES, transcendentals=0
        ),
        name="edges",
    )(in_vmem(advected), halo_x, halo_y, inflow[None, :], edge_x, edge_y)
    fresh, fields = pl.pallas_call(
        lambda *refs: relax_kernel(wx, wy, *refs),
        out_shape=(
            jax.ShapeDtypeStruct((9, n, LANES), F32),
            jax.ShapeDtypeStruct((45, wx, wy), F32),
        ),
        in_specs=[whole] * 6,
        out_specs=(anywhere, whole),
        scratch_shapes=[
            pltpu.VMEM((9, COEF_ROWS, n), F32),
            pltpu.VMEM((48, n), F32),
            pltpu.VMEM((9, n, LANES), F32),
            pltpu.SemaphoreType.DMA((9,)),
        ],
        compiler_params=pltpu.CompilerParams(vmem_limit_bytes=16 << 20),
        name="relax",
    )(
        total,
        other,
        masks,
        table,
        in_vmem(advected),
        in_vmem(held),
    )
    return (fresh.reshape(dist.shape), fields.reshape(5, 3, 3, wx, wy))


def solution(mesh):
    in_specs = (P(None, None, "gx", "gy", "vel"), P(), P("vel"))
    out_specs = (P(None, None, "gx", "gy", "vel"), P(None, None, None, "gx", "gy"))
    return jax.shard_map(shards, mesh=mesh, in_specs=in_specs, out_specs=out_specs, check_vma=False)
```

```python
import math

import jax
import jax.numpy as jnp
import ml_dtypes
import numpy as np
from jax import lax
from jax.experimental import pallas as pl
from jax.experimental.pallas import tpu as pltpu
from jax.sharding import PartitionSpec as P

NV = 16
SPACING = 10.0 / NV
VEL_MAX = 5.0
RAREFACTION = 0.25
TIME_STEP = 0.08
WEIGHT = SPACING**3 / (2.0 * math.pi) ** 1.5

LANES = NV * NV
HALF = LANES // 2
SUM_ROWS = 208
TAIL = 160
COEF_ROWS = 32
MASK_ROWS = 16
GROUPS = [(0, 3), (3, 6), (6, 9)]
CHUNKS = 4
F32 = jnp.float32
BF16 = jnp.bfloat16


def levels():
    return (np.arange(NV) + 0.5) * SPACING - VEL_MAX


def lane_speeds():
    return np.repeat(levels(), NV), np.tile(levels(), NV)


def wall_scale():
    level = levels()
    gauss = np.exp(-0.5 * level * level)
    return float(WEIGHT * np.sum(np.maximum(-level, 0.0) * gauss) * np.sum(gauss) ** 2)


def pieces(value, count):
    out = []
    for _ in range(count):
        piece = value.astype(ml_dtypes.bfloat16).astype(np.float64)
        out.append(piece)
        value = value - piece
    return out


def spread_weights():
    vy, vz = lane_speeds()
    square = vy * vy + vz * vz
    wall = np.exp(-0.5 * square)
    table = np.zeros((COEF_ROWS, 2 * LANES + HALF))
    high, low = pieces(square, 2)
    for row in range(3):
        table[row, :LANES] = 1.0
        table[3 + row, :LANES] = vy
        table[6 + row, :LANES] = vz
        table[9 + row, :LANES] = high
        table[12 + row, :LANES] = low
    table[15:17, 2 * LANES :] = 1.0
    for base, shape in (
        (17, wall),
        (20, np.maximum(vy, 0.0) * wall),
        (23, np.maximum(-vy, 0.0) * wall),
    ):
        first, second = pieces(shape, 2)
        table[base, LANES : 2 * LANES] = first
        table[base + 1, LANES : 2 * LANES] = second
        table[base + 2, LANES : 2 * LANES] = first
    return jnp.asarray(table.astype(ml_dtypes.bfloat16))


def own_speed():
    level = lax.axis_index("vel")
    return level, (level.astype(F32) + 0.5) * SPACING - VEL_MAX


def lane_axis(shape, axis):
    return lax.broadcasted_iota(jnp.int32, shape, axis)


def moment_weights():
    row = lane_axis((16, LANES), 0)
    lane = lane_axis((16, LANES), 1)
    vy = ((lane // NV).astype(F32) + 0.5) * SPACING - VEL_MAX
    vz = ((lane % NV).astype(F32) + 0.5) * SPACING - VEL_MAX
    square = vy * vy + vz * vz
    high = square.astype(BF16).astype(F32)
    table = jnp.zeros((16, LANES), F32)
    for at, value in enumerate(
        (1.0, vy, vz, high, square - high, jnp.maximum(-vy, 0.0), jnp.maximum(vy, 0.0))
    ):
        table = jnp.where(row == at, value, table)
    return table.astype(BF16)


def kind_masks(kinds, masks, wx, wy, forward):
    n = wx * wy
    size_y, size_x = kinds.shape
    start_x = lax.axis_index("gx") * wx
    start_y = lax.axis_index("gy") * wy
    behind = jnp.where(forward, 1, -1)
    kind = kinds[...].astype(F32).astype(BF16)
    x = lane_axis((size_x, n), 0)
    own_x = start_x + lane_axis((size_x, n), 1) // wy
    y = lane_axis((size_y, n), 0)
    own_y = start_y + lane_axis((size_y, n), 1) % wy

    def pick(column):
        chosen = jnp.where(x == column, 1.0, 0.0).astype(BF16)
        return jnp.dot(kind, chosen, preferred_element_type=F32)

    def at(table, row):
        return jnp.sum(jnp.where(y == row, table, 0.0), axis=0, keepdims=True)

    here = pick(own_x)
    fluid = 1.0 - at(here, own_y)
    solid_x = at(pick(own_x - behind), own_y)
    solid_b = at(here, own_y - 1)
    solid_a = at(here, own_y + 1)
    column, row = own_x[0:1], own_y[0:1]
    last_x = jnp.logical_and(jnp.logical_not(forward), column == size_x - 1)
    inner_x = jnp.where(last_x, 0.0, fluid)
    inner_b = jnp.where(row == 0, 0.0, fluid)
    inner_a = jnp.where(row == size_y - 1, 0.0, fluid)
    masks[...] = jnp.zeros_like(masks)
    for at_row, value in enumerate(
        (
            fluid,
            inner_x * (1.0 - solid_x),
            inner_x,
            inner_b * (1.0 - solid_b),
            inner_b,
            inner_a * (1.0 - solid_a),
            inner_a,
            fluid * solid_x,
            fluid * solid_b,
            fluid * solid_a,
        )
    ):
        masks[at_row : at_row + 1, :] = value


def moments_kernel(wx, wy, dist, kinds, sums, face_x, face_y, masks, dv, kind, sems):
    n = wx * wy
    copies = {
        first: pltpu.make_async_copy(dist.at[first:last], dv.at[first:last], sems.at[first])
        for first, last in GROUPS
    }
    kind_copy = pltpu.make_async_copy(kinds, kind, sems.at[9])
    kind_copy.start()
    for copy in copies.values():
        copy.start()
    level, vx = own_speed()
    sums[...] = jnp.zeros_like(sums)
    table = moment_weights()
    kind_copy.wait()
    kind_masks(kind, masks, wx, wy, level >= NV // 2)
    forward = level >= NV // 2
    contract = (((1,), (1,)), ((), ()))

    def put(first, step, row):
        for c in range(n // HALF):
            at = first + c * step
            sums[at : at + 1, :] = row[:, c * HALF : (c + 1) * HALF]

    walls_x, walls_y = [None] * 3, [None] * 3
    for k in range(9):
        i, j = divmod(k, 3)
        if k in copies:
            copies[k].wait()
        plane = dv[k]
        high = plane.astype(BF16)
        low = (plane - high.astype(F32)).astype(BF16)
        part = lax.dot_general(table, high, contract, preferred_element_type=F32)
        part = part + lax.dot_general(table, low, contract, preferred_element_type=F32)
        part = part * WEIGHT
        total = part[0:1]
        rows = (
            total,
            vx * total,
            part[1:2],
            part[2:3],
            0.5 * (vx * vx * total + part[3:4] + part[4:5]),
        )
        for f, row in enumerate(rows):
            if k < 8:
                put(f * 32 + k, 8, row)
            else:
                put(TAIL + f * 4, 1, row)
        if i == 0:
            walls_x[j] = total
        if i == 2:
            put(TAIL + (5 + j) * 4, 1, jnp.abs(vx) * jnp.where(forward, total, walls_x[j]))
        if j == 0:
            walls_y[i] = part[5:6] * masks[8:9, :]
        if j == 2:
            put(TAIL + (8 + i) * 4, 1, walls_y[i] + part[6:7] * masks[9:10, :])

    @pl.when(level >= NV // 2)
    def _():
        for j in range(3):
            face_x[j] = dv[6 + j, n - wy : n, :]

    @pl.when(level < NV // 2)
    def _():
        for j in range(3):
            face_x[j] = dv[j, 0:wy, :]

    @pl.when(lax.axis_index("gy") == 0)
    def _():
        for i in range(3):
            for p in range(wx):
                at = p * wy + wy - 1
                face_y[i, p : p + 1, :] = dv[3 * i + 2, at : at + 1, HALF:]

    @pl.when(lax.axis_index("gy") != 0)
    def _():
        for i in range(3):
            for p in range(wx):
                at = p * wy
                face_y[i, p : p + 1, :] = dv[3 * i, at : at + 1, :HALF]


def advect_kernel(wx, wy, dist, table, masks, out, dv, edge_x, edge_y, weights, spread, sems):
    level, vx = own_speed()
    keep = pltpu.make_async_copy(table, weights, sems.at[CHUNKS])
    keep.start()
    row = lane_axis((MASK_ROWS, 7 * HALF), 0)
    column = lane_axis((MASK_ROWS, 7 * HALF), 1)
    select = jnp.where(column // HALF == row, 1.0, 0.0).astype(BF16)
    cx = -TIME_STEP * vx
    face_cx = 6.0 * TIME_STEP * jnp.abs(vx)
    lane = lane_axis((1, HALF), 1)
    q = lane_axis((wy, HALF), 0)

    def speed_y(half):
        return ((lane // NV + half * (NV // 2)).astype(F32) + 0.5) * SPACING - VEL_MAX

    def differences(a):
        four = 4.0 * a[1]
        rest = four - (a[0] + a[2])
        return rest - 2.0 * a[0], a[2] - a[0], 2.0 * a[2] - rest

    def tile(p, half, sign, trace):
        rows = pl.ds(pl.multiple_of(p * wy, wy), wy)
        lanes = slice(half * HALF, (half + 1) * HALF)
        vy = speed_y(half)
        cy = -TIME_STEP * vy
        face_cy = 6.0 * TIME_STEP * jnp.abs(vy)
        d = [[dv[3 * i + j, rows, lanes] for j in range(3)] for i in range(3)]
        fluid, wall_x, own_x, wall_b, own_b, wall_a, own_a = [
            spread[rows, m * HALF : (m + 1) * HALF] for m in range(7)
        ]
        dx = [differences([d[i][j] for i in range(3)]) for j in range(3)]
        for i in range(3):
            dy = differences(d[i])
            for j in range(3):
                value = d[i][j] + fluid * (cx * dx[j][i] + cy * dy[j])
                if i == (0 if sign > 0 else 2):
                    change = own_x * d[i][j]
                    if trace is not None:
                        change = change - wall_x * trace(j, lanes)
                    value = value - face_cx * change
                if half == 1 and j == 0:
                    raw = jnp.where(q == 0, 0.0, pltpu.roll(d[i][2], 1, 0))
                    value = value + face_cy * (wall_b * raw - own_b * d[i][j])
                if half == 0 and j == 2:
                    raw = jnp.where(q == wy - 1, 0.0, pltpu.roll(d[i][0], wy - 1, 0))
                    value = value + face_cy * (wall_a * raw - own_a * d[i][j])
                out[3 * i + j, rows, lanes] = value

    def sweep(sign):
        edge = 0 if sign > 0 else wx - 1
        source = 6 if sign > 0 else 0
        share = wx // CHUNKS
        order = range(CHUNKS) if sign > 0 else range(CHUNKS)[::-1]

        def part(chunk):
            rows = slice(chunk * share * wy, (chunk + 1) * share * wy)
            return pltpu.make_async_copy(dist.at[:, rows], dv.at[:, rows], sems.at[chunk])

        for chunk in order:
            part(chunk).start()
        spread[...] = lax.dot_general(
            masks[...].astype(BF16), select, (((0,), (0,)), ((), ())), preferred_element_type=F32
        )
        edge_x[...] = face_cx * spread[edge * wy : (edge + 1) * wy, HALF : 2 * HALF]
        for chunk in order:
            part(chunk).wait()
            low, high = chunk * share, (chunk + 1) * share
            if chunk == order[0]:
                for half in range(2):
                    tile(edge, half, sign, None)
                low, high = (low + 1, high) if sign > 0 else (low, high - 1)

            @pl.loop(low, high)
            def _(p):
                behind = pl.ds(pl.multiple_of((p - sign) * wy, wy), wy)
                for half in range(2):
                    tile(p, half, sign, lambda j, lanes: dv[source + j, behind, lanes])

    @pl.when(level >= NV // 2)
    def _():
        sweep(1)

    @pl.when(level < NV // 2)
    def _():
        sweep(-1)

    upper = lax.axis_index("gy") != 0

    @pl.when(upper)
    def _():
        for p in range(wx):
            at = p * wy
            edge_y[p : p + 1, :] = spread[at : at + 1, 3 * HALF : 4 * HALF] * (
                6.0 * TIME_STEP * speed_y(1)
            )

    @pl.when(jnp.logical_not(upper))
    def _():
        for p in range(wx):
            at = p * wy + wy - 1
            edge_y[p : p + 1, :] = spread[at : at + 1, 5 * HALF : 6 * HALF] * (
                -6.0 * TIME_STEP * speed_y(0)
            )

    keep.wait()


def edges_kernel(wx, wy, inside, halo_x, inflow, edge_x, out):
    del inside
    level, _ = own_speed()
    forward = level >= NV // 2
    first_x = lax.axis_index("gx") == 0

    def along_x(p, i, outside):
        rows = slice(p * wy, (p + 1) * wy)
        for j in range(3):
            for half in range(2):
                lanes = slice(half * HALF, (half + 1) * HALF)
                out[3 * i + j, rows, lanes] += edge_x[...] * outside(j, lanes)

    @pl.when(forward)
    def _():
        along_x(0, 0, lambda j, at: jnp.where(first_x, inflow[:, at], halo_x[j, :, at]))

    @pl.when(jnp.logical_not(forward))
    def _():
        along_x(wx - 1, 2, lambda j, at: halo_x[j, :, at])


def rows_kernel(wx, wy, inside, rows, halo_y, edge_y, out, fresh, sem):
    del inside
    upper = lax.axis_index("gy") != 0

    def write(row, first, face, half):
        fresh[...] = rows[...]
        for i in range(3):
            for p in range(wx):
                fresh[i, p, row : row + 1, :] += edge_y[p : p + 1, :] * halo_y[i, p : p + 1, :]
        lanes = slice(half * HALF, (half + 1) * HALF)
        copies = [
            pltpu.make_async_copy(
                fresh.at[i], out.at[3 * i + face, :, first : first + 8, lanes], sem.at[i]
            )
            for i in range(3)
        ]
        for copy in copies:
            copy.start()
        for copy in copies:
            copy.wait()

    @pl.when(upper)
    def _():
        write(0, 0, 0, 1)

    @pl.when(jnp.logical_not(upper))
    def _():
        write(7, wy - 8, 2, 0)


def split(value, count):
    out = []
    for _ in range(count):
        piece = value.astype(BF16).astype(F32)
        out.append(piece)
        value = value - piece
    return out


def relax_kernel(
    wx,
    wy,
    sums_a,
    sums_b,
    masks,
    table,
    advected,
    dv,
    out,
    fields_out,
    border,
    coef,
    fields,
    result,
    sems,
):
    n = wx * wy
    level, vx = own_speed()
    is_forward = level >= NV // 2
    parts = range(n // HALF)

    def wide(read, first, step, count):
        return jnp.concatenate(
            [read(slice(first + c * step, first + c * step + count)) for c in parts], axis=1
        )

    def both(rows):
        return sums_a[rows, :] + sums_b[rows, :]

    def received(rows):
        return sums_b[rows, :]

    fluid = masks[0:1, :]
    coef[...] = jnp.zeros_like(coef)
    log2e = math.log2(math.e)

    def store(planes, start, value, count):
        for piece_at, piece in enumerate(split(value, count)):
            coef[planes, start + piece_at, :] = piece

    for planes, where, s in (
        (slice(0, 8), 0, [wide(both, f * 32, 8, 8) for f in range(5)]),
        (slice(8, 9), 8, [wide(both, TAIL + f * 4, 1, 1) for f in range(5)]),
    ):
        rho = s[0]
        ux, uy, uz = s[1] / rho, s[2] / rho, s[3] / rho
        temp = 2.0 / 3.0 * (s[4] / rho - 0.5 * (ux * ux + uy * uy + uz * uz))
        for f, value in enumerate((rho, ux, uy, uz, temp)):
            at = f * 9 + where
            fields[at : at + value.shape[0], :] = value
        rate = rho * jnp.sqrt(temp) / RAREFACTION * TIME_STEP * fluid
        slope = (0.5 * log2e) / temp
        height = (
            2.0 * jnp.log2(rho)
            - jnp.log2(temp)
            + math.log2(TIME_STEP / RAREFACTION)
            - slope * ((vx - ux) * (vx - ux) + uy * uy + uz * uz)
        )
        height = jnp.where(fluid == 0.0, -1e30, height)
        store(planes, 0, height, 3)
        store(planes, 3, 2.0 * slope * uy, 3)
        store(planes, 6, 2.0 * slope * uz, 3)
        store(planes, 9, -slope, 3)
        store(planes, 12, -slope, 3)
        store(planes, 15, rate, 2)

    def store_wall(k, start, value):
        first, second = split(value, 2)
        coef[k, start : start + 1, :] = first
        coef[k, start + 1 : start + 2, :] = first
        coef[k, start + 2 : start + 3, :] = second

    scale = 6.0 * TIME_STEP / wall_scale()
    forward = is_forward.astype(F32)
    gauss_x = jnp.exp(jnp.full((1, n), -0.5, F32) * (vx * vx)) * scale
    solid_x = masks[7:8, :] * gauss_x * jnp.abs(vx)
    solid_b = masks[8:9, :] * gauss_x
    solid_a = masks[9:10, :] * gauss_x
    for j in range(3):
        value = solid_x * wide(received, TAIL + (5 + j) * 4, 1, 1)
        store_wall(j, 17, value * forward)
        store_wall(6 + j, 17, value * (1.0 - forward))
    for i in range(3):
        value = wide(both, TAIL + (8 + i) * 4, 1, 1)
        store_wall(3 * i, 20, solid_b * value)
        store_wall(3 * i + 2, 23, solid_a * value)

    weights = table[...]
    chunk = 128
    block = 2 * chunk
    copies = []
    for k in range(9):
        for start in range(0, n, chunk):
            rows = slice(start, start + chunk)
            spread = lax.dot_general(
                coef[k, :, rows].astype(BF16),
                weights,
                (((0,), (0,)), ((), ())),
                preferred_element_type=F32,
            )
            rate = spread[:, 2 * LANES :]
            for half in range(2):
                lanes = slice(half * HALF, (half + 1) * HALF)
                target = jnp.exp2(spread[:, lanes])
                wall = spread[:, LANES + half * HALF : LANES + (half + 1) * HALF]
                result[k, rows, lanes] = (
                    advected[k, rows, lanes] - rate * dv[k, rows, lanes] + (target + wall)
                )
            if (start + chunk) % block == 0:
                done = slice(start + chunk - block, start + chunk)
                copy = pltpu.make_async_copy(
                    result.at[k, done], out.at[k, done], sems.at[len(copies)]
                )
                copy.start()
                copies.append(copy)
    upper = lax.axis_index("gy") != 0

    def keep(first, face, half):
        for i in range(3):
            for p in range(wx):
                at = slice(p * wy + first, p * wy + first + 8)
                border[i, p] = result[3 * i + face, at, half * HALF : (half + 1) * HALF]

    @pl.when(upper)
    def _():
        keep(0, 0, 1)

    @pl.when(jnp.logical_not(upper))
    def _():
        keep(wy - 8, 2, 0)

    for p in range(wx):
        fields_out[:, p, :] = fields[0:45, p * wy : (p + 1) * wy]
    for copy in copies:
        copy.wait()


def exchanges():
    count = lax.axis_size("vel")
    return (
        [(v, v ^ 1) for v in range(count)],
        [(v, v ^ 3) for v in range(count)],
        [(v, v ^ 4) for v in range(count)],
        [(v, v ^ 8) for v in range(count)],
    )


def upwind_pairs():
    count = lax.axis_size("gx")
    pairs = []
    for v in range(lax.axis_size("vel")):
        step = 1 if v >= NV // 2 else -1
        for g in range(count):
            if 0 <= g + step < count:
                pairs.append((v * count + g, v * count + g + step))
    return pairs


def vmem(shape):
    return pltpu.VMEM(shape, F32)


def in_vmem(x):
    return pltpu.with_memory_space_constraint(x, pltpu.VMEM)


def shards(dist, cell_kind, inflow):
    wx, wy = dist.shape[2], dist.shape[3]
    n = wx * wy
    whole = pl.BlockSpec(memory_space=pltpu.VMEM)
    anywhere = pl.BlockSpec(memory_space=pl.ANY)
    planes = pltpu.with_memory_space_constraint(dist.reshape(9, n, LANES), pltpu.HBM)
    sums, face_x, face_y, masks = pl.pallas_call(
        lambda *refs: moments_kernel(wx, wy, *refs),
        out_shape=(
            vmem((SUM_ROWS, HALF)),
            vmem((3, wy, LANES)),
            vmem((3, wx, HALF)),
            vmem((MASK_ROWS, n)),
        ),
        in_specs=[anywhere, anywhere],
        out_specs=(whole, whole, whole, whole),
        scratch_shapes=[
            pltpu.VMEM((9, n, LANES), F32),
            pltpu.VMEM(cell_kind.shape[::-1], jnp.int32),
            pltpu.SemaphoreType.DMA((10,)),
        ],
        compiler_params=pltpu.CompilerParams(vmem_limit_bytes=16 << 20),
        cost_estimate=pl.CostEstimate(
            flops=2 * 32 * 9 * n * LANES, bytes_accessed=4 * 9 * n * LANES, transcendentals=0
        ),
        name="moments",
    )(planes, pltpu.with_memory_space_constraint(cell_kind.T, pltpu.HBM))
    table = spread_weights()
    advected, held, edge_x, edge_y, table = pl.pallas_call(
        lambda *refs: advect_kernel(wx, wy, *refs),
        out_shape=(
            vmem((9, n, LANES)),
            vmem((9, n, LANES)),
            vmem((wy, HALF)),
            vmem((wx, HALF)),
            pltpu.VMEM(table.shape, table.dtype),
        ),
        in_specs=[anywhere, anywhere, whole],
        out_specs=(whole,) * 5,
        scratch_shapes=[pltpu.VMEM((n, 7 * HALF), F32), pltpu.SemaphoreType.DMA((CHUNKS + 1,))],
        compiler_params=pltpu.CompilerParams(vmem_limit_bytes=8 << 20),
        cost_estimate=pl.CostEstimate(
            flops=20 * 9 * n * LANES, bytes_accessed=12 * 9 * n * LANES, transcendentals=0
        ),
        name="advect",
    )(planes, pltpu.with_memory_space_constraint(table, pltpu.HBM), masks)
    steps = exchanges()
    total = sums + lax.ppermute(sums, "vel", steps[0])
    total = total + lax.ppermute(total, "vel", steps[1])
    total, edge_x, edge_y = lax.optimization_barrier((total, edge_x, edge_y))
    halo_x = lax.ppermute(face_x, ("vel", "gx"), upwind_pairs())
    total = total + lax.ppermute(total, "vel", steps[2])
    total, halo_x = lax.optimization_barrier((total, halo_x))
    advected = pl.pallas_call(
        lambda *refs: edges_kernel(wx, wy, *refs),
        out_shape=vmem((9, n, LANES)),
        in_specs=[whole] * 4,
        out_specs=whole,
        input_output_aliases={0: 0},
        compiler_params=pltpu.CompilerParams(vmem_limit_bytes=4 << 20),
        name="edges",
    )(in_vmem(advected), halo_x, inflow[None, :], edge_x)
    other = lax.ppermute(total, "vel", steps[3])
    halo_y = lax.ppermute(face_y, "gy", [(0, 1), (1, 0)])
    fresh, fields, border = pl.pallas_call(
        lambda *refs: relax_kernel(wx, wy, *refs),
        out_shape=(
            jax.ShapeDtypeStruct((9, n, LANES), F32),
            jax.ShapeDtypeStruct((45, wx, wy), F32),
            vmem((3, wx, 8, HALF)),
        ),
        in_specs=[whole] * 6,
        out_specs=(anywhere, whole, whole),
        scratch_shapes=[
            pltpu.VMEM((9, COEF_ROWS, n), F32),
            pltpu.VMEM((48, n), F32),
            pltpu.VMEM((9, n, LANES), F32),
            pltpu.SemaphoreType.DMA((9 * n // 256,)),
        ],
        compiler_params=pltpu.CompilerParams(vmem_limit_bytes=16 << 20),
        name="relax",
    )(total, other, masks, table, in_vmem(advected), in_vmem(held))
    fresh = pl.pallas_call(
        lambda *refs: rows_kernel(wx, wy, *refs),
        out_shape=jax.ShapeDtypeStruct((9, wx, wy, LANES), F32),
        in_specs=[anywhere, whole, whole, whole],
        out_specs=anywhere,
        scratch_shapes=[pltpu.VMEM((3, wx, 8, HALF), F32), pltpu.SemaphoreType.DMA((3,))],
        input_output_aliases={0: 0},
        compiler_params=pltpu.CompilerParams(vmem_limit_bytes=4 << 20),
        name="rows",
    )(fresh.reshape(9, wx, wy, LANES), border, halo_y, edge_y)
    return (fresh.reshape(dist.shape), fields.reshape(5, 3, 3, wx, wy))


def solution(mesh):
    in_specs = (P(None, None, "gx", "gy", "vel"), P(), P("vel"))
    out_specs = (P(None, None, "gx", "gy", "vel"), P(None, None, None, "gx", "gy"))
    return jax.shard_map(shards, mesh=mesh, in_specs=in_specs, out_specs=out_specs, check_vma=False)
```

```python
import math

import jax
import jax.numpy as jnp
import ml_dtypes
import numpy as np
from jax import lax
from jax.experimental import pallas as pl
from jax.experimental.pallas import tpu as pltpu
from jax.sharding import PartitionSpec as P

NV = 16
SPACING = 10.0 / NV
VEL_MAX = 5.0
RAREFACTION = 0.25
TIME_STEP = 0.08
WEIGHT = SPACING**3 / (2.0 * math.pi) ** 1.5

LANES = NV * NV
HALF = LANES // 2
SUM_ROWS = 208
TAIL = 160
COEF_ROWS = 32
MASK_ROWS = 16
GROUPS = [(0, 3), (3, 6), (6, 9)]
ORDERS = ((1, 3, 4, 8), (4, 8, 1, 3))
SLOT = slice(TAIL + 20, TAIL + 32)
CHUNKS = 4
F32 = jnp.float32
BF16 = jnp.bfloat16


def levels():
    return (np.arange(NV) + 0.5) * SPACING - VEL_MAX


def lane_speeds():
    return np.repeat(levels(), NV), np.tile(levels(), NV)


def wall_scale():
    level = levels()
    gauss = np.exp(-0.5 * level * level)
    return float(WEIGHT * np.sum(np.maximum(-level, 0.0) * gauss) * np.sum(gauss) ** 2)


def pieces(value, count):
    out = []
    for _ in range(count):
        piece = value.astype(ml_dtypes.bfloat16).astype(np.float64)
        out.append(piece)
        value = value - piece
    return out


def spread_weights():
    vy, vz = lane_speeds()
    square = vy * vy + vz * vz
    wall = np.exp(-0.5 * square)
    table = np.zeros((COEF_ROWS, 2 * LANES + HALF))
    high, low = pieces(square, 2)
    for row in range(3):
        table[row, :LANES] = 1.0
        table[3 + row, :LANES] = vy
        table[6 + row, :LANES] = vz
        table[9 + row, :LANES] = high
        table[12 + row, :LANES] = low
    table[15:17, 2 * LANES :] = 1.0
    for base, shape in (
        (17, wall),
        (20, np.maximum(vy, 0.0) * wall),
        (23, np.maximum(-vy, 0.0) * wall),
    ):
        first, second = pieces(shape, 2)
        table[base, LANES : 2 * LANES] = first
        table[base + 1, LANES : 2 * LANES] = second
        table[base + 2, LANES : 2 * LANES] = first
    return jnp.asarray(table.astype(ml_dtypes.bfloat16))


def own_speed():
    level = lax.axis_index("vel")
    return level, (level.astype(F32) + 0.5) * SPACING - VEL_MAX


def lane_axis(shape, axis):
    return lax.broadcasted_iota(jnp.int32, shape, axis)


def moment_weights():
    row = lane_axis((16, LANES), 0)
    lane = lane_axis((16, LANES), 1)
    vy = ((lane // NV).astype(F32) + 0.5) * SPACING - VEL_MAX
    vz = ((lane % NV).astype(F32) + 0.5) * SPACING - VEL_MAX
    square = vy * vy + vz * vz
    high = square.astype(BF16).astype(F32)
    table = jnp.zeros((16, LANES), F32)
    for at, value in enumerate(
        (1.0, vy, vz, high, square - high, jnp.maximum(-vy, 0.0), jnp.maximum(vy, 0.0))
    ):
        table = jnp.where(row == at, value, table)
    return table.astype(BF16)


def kind_masks(kinds, masks, wx, wy, forward):
    n = wx * wy
    size_y, size_x = kinds.shape
    start_x = lax.axis_index("gx") * wx
    start_y = lax.axis_index("gy") * wy
    behind = jnp.where(forward, 1, -1)
    kind = kinds[...].astype(F32).astype(BF16)
    x = lane_axis((size_x, n), 0)
    own_x = start_x + lane_axis((size_x, n), 1) // wy
    y = lane_axis((size_y, n), 0)
    own_y = start_y + lane_axis((size_y, n), 1) % wy

    def pick(column):
        chosen = jnp.where(x == column, 1.0, 0.0).astype(BF16)
        return jnp.dot(kind, chosen, preferred_element_type=F32)

    def at(table, row):
        return jnp.sum(jnp.where(y == row, table, 0.0), axis=0, keepdims=True)

    here = pick(own_x)
    fluid = 1.0 - at(here, own_y)
    solid_x = at(pick(own_x - behind), own_y)
    solid_b = at(here, own_y - 1)
    solid_a = at(here, own_y + 1)
    column, row = own_x[0:1], own_y[0:1]
    last_x = jnp.logical_and(jnp.logical_not(forward), column == size_x - 1)
    inner_x = jnp.where(last_x, 0.0, fluid)
    inner_b = jnp.where(row == 0, 0.0, fluid)
    inner_a = jnp.where(row == size_y - 1, 0.0, fluid)
    masks[...] = jnp.zeros_like(masks)
    for at_row, value in enumerate(
        (
            fluid,
            inner_x * (1.0 - solid_x),
            inner_x,
            inner_b * (1.0 - solid_b),
            inner_b,
            inner_a * (1.0 - solid_a),
            inner_a,
            fluid * solid_x,
            fluid * solid_b,
            fluid * solid_a,
        )
    ):
        masks[at_row : at_row + 1, :] = value


def moments_kernel(wx, wy, dist, kinds, sums, face_x, face_y, masks, dv, kind, sems):
    n = wx * wy
    copies = {
        first: pltpu.make_async_copy(dist.at[first:last], dv.at[first:last], sems.at[first])
        for first, last in GROUPS
    }
    kind_copy = pltpu.make_async_copy(kinds, kind, sems.at[9])
    kind_copy.start()
    for copy in copies.values():
        copy.start()
    level, vx = own_speed()
    sums[...] = jnp.zeros_like(sums)
    table = moment_weights()
    kind_copy.wait()
    kind_masks(kind, masks, wx, wy, level >= NV // 2)
    forward = level >= NV // 2
    contract = (((1,), (1,)), ((), ()))

    def put(first, step, row):
        for c in range(n // HALF):
            at = first + c * step
            sums[at : at + 1, :] = row[:, c * HALF : (c + 1) * HALF]

    walls_x, walls_y = [None] * 3, [None] * 3
    for k in range(9):
        i, j = divmod(k, 3)
        if k in copies:
            copies[k].wait()
        plane = dv[k]
        high = plane.astype(BF16)
        low = (plane - high.astype(F32)).astype(BF16)
        part = lax.dot_general(table, high, contract, preferred_element_type=F32)
        part = part + lax.dot_general(table, low, contract, preferred_element_type=F32)
        part = part * WEIGHT
        total = part[0:1]
        rows = (
            total,
            vx * total,
            part[1:2],
            part[2:3],
            0.5 * (vx * vx * total + part[3:4] + part[4:5]),
        )
        for f, row in enumerate(rows):
            if k < 8:
                put(f * 32 + k, 8, row)
            else:
                put(TAIL + f * 4, 1, row)
        if i == 0:
            walls_x[j] = total
        if i == 2:
            put(TAIL + (5 + j) * 4, 1, jnp.abs(vx) * jnp.where(forward, total, walls_x[j]))
        if j == 0:
            walls_y[i] = part[5:6] * masks[8:9, :]
        if j == 2:
            put(TAIL + (8 + i) * 4, 1, walls_y[i] + part[6:7] * masks[9:10, :])

    @pl.when(level >= NV // 2)
    def _():
        for j in range(3):
            face_x[j] = dv[6 + j, n - wy : n, :]

    @pl.when(level < NV // 2)
    def _():
        for j in range(3):
            face_x[j] = dv[j, 0:wy, :]

    @pl.when(lax.axis_index("gy") == 0)
    def _():
        for i in range(3):
            for p in range(wx):
                at = p * wy + wy - 1
                face_y[i, p : p + 1, :] = dv[3 * i + 2, at : at + 1, HALF:]

    @pl.when(lax.axis_index("gy") != 0)
    def _():
        for i in range(3):
            for p in range(wx):
                at = p * wy
                face_y[i, p : p + 1, :] = dv[3 * i, at : at + 1, :HALF]


def advect_kernel(wx, wy, dist, table, masks, out, dv, edge_x, edge_y, weights, spread, sems):
    level, vx = own_speed()
    keep = pltpu.make_async_copy(table, weights, sems.at[CHUNKS])
    keep.start()
    row = lane_axis((MASK_ROWS, 7 * HALF), 0)
    column = lane_axis((MASK_ROWS, 7 * HALF), 1)
    select = jnp.where(column // HALF == row, 1.0, 0.0).astype(BF16)
    cx = -TIME_STEP * vx
    face_cx = 6.0 * TIME_STEP * jnp.abs(vx)
    lane = lane_axis((1, HALF), 1)
    q = lane_axis((wy, HALF), 0)

    def speed_y(half):
        return ((lane // NV + half * (NV // 2)).astype(F32) + 0.5) * SPACING - VEL_MAX

    def differences(a):
        four = 4.0 * a[1]
        rest = four - (a[0] + a[2])
        return rest - 2.0 * a[0], a[2] - a[0], 2.0 * a[2] - rest

    def tile(p, half, sign, trace):
        rows = pl.ds(pl.multiple_of(p * wy, wy), wy)
        lanes = slice(half * HALF, (half + 1) * HALF)
        vy = speed_y(half)
        cy = -TIME_STEP * vy
        face_cy = 6.0 * TIME_STEP * jnp.abs(vy)
        d = [[dv[3 * i + j, rows, lanes] for j in range(3)] for i in range(3)]
        fluid, wall_x, own_x, wall_b, own_b, wall_a, own_a = [
            spread[rows, m * HALF : (m + 1) * HALF] for m in range(7)
        ]
        dx = [differences([d[i][j] for i in range(3)]) for j in range(3)]
        for i in range(3):
            dy = differences(d[i])
            for j in range(3):
                value = d[i][j] + fluid * (cx * dx[j][i] + cy * dy[j])
                if i == (0 if sign > 0 else 2):
                    change = own_x * d[i][j]
                    if trace is not None:
                        change = change - wall_x * trace(j, lanes)
                    value = value - face_cx * change
                if half == 1 and j == 0:
                    raw = jnp.where(q == 0, 0.0, pltpu.roll(d[i][2], 1, 0))
                    value = value + face_cy * (wall_b * raw - own_b * d[i][j])
                if half == 0 and j == 2:
                    raw = jnp.where(q == wy - 1, 0.0, pltpu.roll(d[i][0], wy - 1, 0))
                    value = value + face_cy * (wall_a * raw - own_a * d[i][j])
                out[3 * i + j, rows, lanes] = value

    def sweep(sign):
        edge = 0 if sign > 0 else wx - 1
        source = 6 if sign > 0 else 0
        share = wx // CHUNKS
        order = range(CHUNKS) if sign > 0 else range(CHUNKS)[::-1]

        def part(chunk):
            rows = slice(chunk * share * wy, (chunk + 1) * share * wy)
            return pltpu.make_async_copy(dist.at[:, rows], dv.at[:, rows], sems.at[chunk])

        for chunk in order:
            part(chunk).start()
        spread[...] = lax.dot_general(
            masks[...].astype(BF16), select, (((0,), (0,)), ((), ())), preferred_element_type=F32
        )
        edge_x[...] = face_cx * spread[edge * wy : (edge + 1) * wy, HALF : 2 * HALF]
        for chunk in order:
            part(chunk).wait()
            low, high = chunk * share, (chunk + 1) * share
            if chunk == order[0]:
                for half in range(2):
                    tile(edge, half, sign, None)
                low, high = (low + 1, high) if sign > 0 else (low, high - 1)

            @pl.loop(low, high)
            def _(p):
                behind = pl.ds(pl.multiple_of((p - sign) * wy, wy), wy)
                for half in range(2):
                    tile(p, half, sign, lambda j, lanes: dv[source + j, behind, lanes])

    @pl.when(level >= NV // 2)
    def _():
        sweep(1)

    @pl.when(level < NV // 2)
    def _():
        sweep(-1)

    upper = lax.axis_index("gy") != 0

    @pl.when(upper)
    def _():
        for p in range(wx):
            at = p * wy
            edge_y[p : p + 1, :] = spread[at : at + 1, 3 * HALF : 4 * HALF] * (
                6.0 * TIME_STEP * speed_y(1)
            )

    @pl.when(jnp.logical_not(upper))
    def _():
        for p in range(wx):
            at = p * wy + wy - 1
            edge_y[p : p + 1, :] = spread[at : at + 1, 5 * HALF : 6 * HALF] * (
                -6.0 * TIME_STEP * speed_y(0)
            )

    keep.wait()


def edges_kernel(wx, wy, inside, halo_x, inflow, edge_x, out):
    del inside
    level, _ = own_speed()
    forward = level >= NV // 2
    first_x = lax.axis_index("gx") == 0

    def along_x(p, i, outside):
        rows = slice(p * wy, (p + 1) * wy)
        for j in range(3):
            for half in range(2):
                lanes = slice(half * HALF, (half + 1) * HALF)
                out[3 * i + j, rows, lanes] += edge_x[...] * outside(j, lanes)

    @pl.when(forward)
    def _():
        along_x(0, 0, lambda j, at: jnp.where(first_x, inflow[:, at], halo_x[j, :, at]))

    @pl.when(jnp.logical_not(forward))
    def _():
        along_x(wx - 1, 2, lambda j, at: halo_x[j, :, at])


def rows_kernel(wx, wy, inside, rows, halo_y, edge_y, out, fresh, sem):
    del inside
    upper = lax.axis_index("gy") != 0

    def write(row, first, face, half):
        fresh[...] = rows[...]
        for i in range(3):
            for p in range(wx):
                fresh[i, p, row : row + 1, :] += edge_y[p : p + 1, :] * halo_y[i, p : p + 1, :]
        lanes = slice(half * HALF, (half + 1) * HALF)
        copies = [
            pltpu.make_async_copy(
                fresh.at[i], out.at[3 * i + face, :, first : first + 8, lanes], sem.at[i]
            )
            for i in range(3)
        ]
        for copy in copies:
            copy.start()
        for copy in copies:
            copy.wait()

    @pl.when(upper)
    def _():
        write(0, 0, 0, 1)

    @pl.when(jnp.logical_not(upper))
    def _():
        write(7, wy - 8, 2, 0)


def split(value, count):
    out = []
    for _ in range(count):
        piece = value.astype(BF16).astype(F32)
        out.append(piece)
        value = value - piece
    return out


def relax_kernel(
    wx,
    wy,
    sums_a,
    sums_b,
    masks,
    table,
    advected,
    dv,
    out,
    fields_out,
    border,
    coef,
    fields,
    result,
    sems,
):
    n = wx * wy
    level, vx = own_speed()
    is_forward = level >= NV // 2
    parts = range(n // HALF)

    def wide(read, first, step, count):
        return jnp.concatenate(
            [read(slice(first + c * step, first + c * step + count)) for c in parts], axis=1
        )

    def both(rows):
        return sums_a[rows, :] + sums_b[rows, :]

    def slot(rows):
        return jnp.where(lax.axis_index("gx") % 2 == 1, both(rows), sums_b[rows, :])

    fluid = masks[0:1, :]
    coef[...] = jnp.zeros_like(coef)
    log2e = math.log2(math.e)

    def store(planes, start, value, count):
        for piece_at, piece in enumerate(split(value, count)):
            coef[planes, start + piece_at, :] = piece

    for planes, where, s in (
        (slice(0, 8), 0, [wide(both, f * 32, 8, 8) for f in range(5)]),
        (slice(8, 9), 8, [wide(both, TAIL + f * 4, 1, 1) for f in range(5)]),
    ):
        rho = s[0]
        ux, uy, uz = s[1] / rho, s[2] / rho, s[3] / rho
        temp = 2.0 / 3.0 * (s[4] / rho - 0.5 * (ux * ux + uy * uy + uz * uz))
        for f, value in enumerate((rho, ux, uy, uz, temp)):
            at = f * 9 + where
            fields[at : at + value.shape[0], :] = value
        rate = rho * jnp.sqrt(temp) / RAREFACTION * TIME_STEP * fluid
        slope = (0.5 * log2e) / temp
        height = (
            2.0 * jnp.log2(rho)
            - jnp.log2(temp)
            + math.log2(TIME_STEP / RAREFACTION)
            - slope * ((vx - ux) * (vx - ux) + uy * uy + uz * uz)
        )
        height = jnp.where(fluid == 0.0, -1e30, height)
        store(planes, 0, height, 3)
        store(planes, 3, 2.0 * slope * uy, 3)
        store(planes, 6, 2.0 * slope * uz, 3)
        store(planes, 9, -slope, 3)
        store(planes, 12, -slope, 3)
        store(planes, 15, rate, 2)

    def store_wall(k, start, value):
        first, second = split(value, 2)
        coef[k, start : start + 1, :] = first
        coef[k, start + 1 : start + 2, :] = first
        coef[k, start + 2 : start + 3, :] = second

    scale = 6.0 * TIME_STEP / wall_scale()
    forward = is_forward.astype(F32)
    gauss_x = jnp.exp(jnp.full((1, n), -0.5, F32) * (vx * vx)) * scale
    solid_x = masks[7:8, :] * gauss_x * jnp.abs(vx)
    solid_b = masks[8:9, :] * gauss_x
    solid_a = masks[9:10, :] * gauss_x
    for j in range(3):
        value = solid_x * wide(slot, TAIL + (5 + j) * 4, 1, 1)
        store_wall(j, 17, value * forward)
        store_wall(6 + j, 17, value * (1.0 - forward))
    for i in range(3):
        value = wide(both, TAIL + (8 + i) * 4, 1, 1)
        store_wall(3 * i, 20, solid_b * value)
        store_wall(3 * i + 2, 23, solid_a * value)

    weights = table[...]
    chunk = 128
    block = 2 * chunk
    copies = []
    for k in range(9):
        for start in range(0, n, chunk):
            rows = slice(start, start + chunk)
            spread = lax.dot_general(
                coef[k, :, rows].astype(BF16),
                weights,
                (((0,), (0,)), ((), ())),
                preferred_element_type=F32,
            )
            rate = spread[:, 2 * LANES :]
            for half in range(2):
                lanes = slice(half * HALF, (half + 1) * HALF)
                target = jnp.exp2(spread[:, lanes])
                wall = spread[:, LANES + half * HALF : LANES + (half + 1) * HALF]
                result[k, rows, lanes] = (
                    advected[k, rows, lanes] - rate * dv[k, rows, lanes] + (target + wall)
                )
            if (start + chunk) % block == 0:
                done = slice(start + chunk - block, start + chunk)
                copy = pltpu.make_async_copy(
                    result.at[k, done], out.at[k, done], sems.at[len(copies)]
                )
                copy.start()
                copies.append(copy)
    upper = lax.axis_index("gy") != 0

    def keep(first, face, half):
        for i in range(3):
            for p in range(wx):
                at = slice(p * wy + first, p * wy + first + 8)
                border[i, p] = result[3 * i + face, at, half * HALF : (half + 1) * HALF]

    @pl.when(upper)
    def _():
        keep(0, 0, 1)

    @pl.when(jnp.logical_not(upper))
    def _():
        keep(wy - 8, 2, 0)

    for p in range(wx):
        fields_out[:, p, :] = fields[0:45, p * wy : (p + 1) * wy]
    for copy in copies:
        copy.wait()


def exchanges():
    count, columns = lax.axis_size("vel"), lax.axis_size("gx")
    return tuple(
        [
            (v * columns + g, (v ^ steps[g % 2]) * columns + g)
            for v in range(count)
            for g in range(columns)
        ]
        for steps in zip(*ORDERS)
    )


def upwind_pairs():
    count = lax.axis_size("gx")
    pairs = []
    for v in range(lax.axis_size("vel")):
        step = 1 if v >= NV // 2 else -1
        for g in range(count):
            if 0 <= g + step < count:
                pairs.append((v * count + g, v * count + g + step))
    return pairs


def vmem(shape):
    return pltpu.VMEM(shape, F32)


def in_vmem(x):
    return pltpu.with_memory_space_constraint(x, pltpu.VMEM)


def shards(dist, cell_kind, inflow):
    wx, wy = dist.shape[2], dist.shape[3]
    n = wx * wy
    whole = pl.BlockSpec(memory_space=pltpu.VMEM)
    anywhere = pl.BlockSpec(memory_space=pl.ANY)
    planes = pltpu.with_memory_space_constraint(dist.reshape(9, n, LANES), pltpu.HBM)
    sums, face_x, face_y, masks = pl.pallas_call(
        lambda *refs: moments_kernel(wx, wy, *refs),
        out_shape=(
            vmem((SUM_ROWS, HALF)),
            vmem((3, wy, LANES)),
            vmem((3, wx, HALF)),
            vmem((MASK_ROWS, n)),
        ),
        in_specs=[anywhere, anywhere],
        out_specs=(whole, whole, whole, whole),
        scratch_shapes=[
            pltpu.VMEM((9, n, LANES), F32),
            pltpu.VMEM(cell_kind.shape[::-1], jnp.int32),
            pltpu.SemaphoreType.DMA((10,)),
        ],
        compiler_params=pltpu.CompilerParams(vmem_limit_bytes=16 << 20),
        cost_estimate=pl.CostEstimate(
            flops=2 * 32 * 9 * n * LANES, bytes_accessed=4 * 9 * n * LANES, transcendentals=0
        ),
        name="moments",
    )(planes, pltpu.with_memory_space_constraint(cell_kind.T, pltpu.HBM))
    table = spread_weights()
    advected, held, edge_x, edge_y, table = pl.pallas_call(
        lambda *refs: advect_kernel(wx, wy, *refs),
        out_shape=(
            vmem((9, n, LANES)),
            vmem((9, n, LANES)),
            vmem((wy, HALF)),
            vmem((wx, HALF)),
            pltpu.VMEM(table.shape, table.dtype),
        ),
        in_specs=[anywhere, anywhere, whole],
        out_specs=(whole,) * 5,
        scratch_shapes=[pltpu.VMEM((n, 7 * HALF), F32), pltpu.SemaphoreType.DMA((CHUNKS + 1,))],
        compiler_params=pltpu.CompilerParams(vmem_limit_bytes=8 << 20),
        cost_estimate=pl.CostEstimate(
            flops=20 * 9 * n * LANES, bytes_accessed=12 * 9 * n * LANES, transcendentals=0
        ),
        name="advect",
    )(planes, pltpu.with_memory_space_constraint(table, pltpu.HBM), masks)
    steps = exchanges()
    def partner(value, pairs):
        return lax.ppermute(value, ("vel", "gx"), pairs)

    odd = lax.axis_index("gx") % 2 == 1
    row = jnp.arange(SUM_ROWS, dtype=jnp.int32)[:, None]
    swapped = jnp.logical_and(odd, jnp.logical_and(row >= SLOT.start, row < SLOT.stop))
    total = sums + partner(sums, steps[0])
    total = jnp.where(swapped, 0.0, total) + partner(total, steps[1])
    halo_x = lax.ppermute(face_x, ("vel", "gx"), upwind_pairs())
    total, halo_x = lax.optimization_barrier((total, halo_x))
    total = total + partner(total, steps[2])
    total, edge_x, edge_y = lax.optimization_barrier((total, edge_x, edge_y))
    advected = pl.pallas_call(
        lambda *refs: edges_kernel(wx, wy, *refs),
        out_shape=vmem((9, n, LANES)),
        in_specs=[whole] * 4,
        out_specs=whole,
        input_output_aliases={0: 0},
        compiler_params=pltpu.CompilerParams(vmem_limit_bytes=4 << 20),
        name="edges",
    )(in_vmem(advected), halo_x, inflow[None, :], edge_x)
    other = partner(total, steps[3])
    halo_y = lax.ppermute(face_y, "gy", [(0, 1), (1, 0)])
    fresh, fields, border = pl.pallas_call(
        lambda *refs: relax_kernel(wx, wy, *refs),
        out_shape=(
            jax.ShapeDtypeStruct((9, n, LANES), F32),
            jax.ShapeDtypeStruct((45, wx, wy), F32),
            vmem((3, wx, 8, HALF)),
        ),
        in_specs=[whole] * 6,
        out_specs=(anywhere, whole, whole),
        scratch_shapes=[
            pltpu.VMEM((9, COEF_ROWS, n), F32),
            pltpu.VMEM((48, n), F32),
            pltpu.VMEM((9, n, LANES), F32),
            pltpu.SemaphoreType.DMA((9 * n // 256,)),
        ],
        compiler_params=pltpu.CompilerParams(vmem_limit_bytes=16 << 20),
        name="relax",
    )(total, other, masks, table, in_vmem(advected), in_vmem(held))
    fresh = pl.pallas_call(
        lambda *refs: rows_kernel(wx, wy, *refs),
        out_shape=jax.ShapeDtypeStruct((9, wx, wy, LANES), F32),
        in_specs=[anywhere, whole, whole, whole],
        out_specs=anywhere,
        scratch_shapes=[pltpu.VMEM((3, wx, 8, HALF), F32), pltpu.SemaphoreType.DMA((3,))],
        input_output_aliases={0: 0},
        compiler_params=pltpu.CompilerParams(vmem_limit_bytes=4 << 20),
        name="rows",
    )(fresh.reshape(9, wx, wy, LANES), border, halo_y, edge_y)
    return (fresh.reshape(dist.shape), fields.reshape(5, 3, 3, wx, wy))


def solution(mesh):
    in_specs = (P(None, None, "gx", "gy", "vel"), P(), P("vel"))
    out_specs = (P(None, None, "gx", "gy", "vel"), P(None, None, None, "gx", "gy"))
    return jax.shard_map(shards, mesh=mesh, in_specs=in_specs, out_specs=out_specs, check_vma=False)
```

```python
import math

import jax
import jax.numpy as jnp
import ml_dtypes
import numpy as np
from jax import lax
from jax.experimental import pallas as pl
from jax.experimental.pallas import tpu as pltpu
from jax.sharding import PartitionSpec as P

NV = 16
SPACING = 10.0 / NV
VEL_MAX = 5.0
RAREFACTION = 0.25
TIME_STEP = 0.08
WEIGHT = SPACING**3 / (2.0 * math.pi) ** 1.5

LANES = NV * NV
HALF = LANES // 2
SUM_ROWS = 208
TAIL = 160
COEF_ROWS = 32
MASK_ROWS = 16
GROUPS = [(0, 3), (3, 6), (6, 9)]
ORDERS = ((1, 3, 4, 8), (4, 8, 1, 3))
SLOT = slice(TAIL + 20, TAIL + 32)
CHUNKS = 4
F32 = jnp.float32
BF16 = jnp.bfloat16


def levels():
    return (np.arange(NV) + 0.5) * SPACING - VEL_MAX


def lane_speeds():
    return np.repeat(levels(), NV), np.tile(levels(), NV)


def wall_scale():
    level = levels()
    gauss = np.exp(-0.5 * level * level)
    return float(WEIGHT * np.sum(np.maximum(-level, 0.0) * gauss) * np.sum(gauss) ** 2)


def pieces(value, count):
    out = []
    for _ in range(count):
        piece = value.astype(ml_dtypes.bfloat16).astype(np.float64)
        out.append(piece)
        value = value - piece
    return out


def spread_weights():
    vy, vz = lane_speeds()
    square = vy * vy + vz * vz
    wall = np.exp(-0.5 * square)
    table = np.zeros((COEF_ROWS, 2 * LANES + HALF))
    high, low = pieces(square, 2)
    for row in range(3):
        table[row, :LANES] = 1.0
        table[3 + row, :LANES] = vy
        table[6 + row, :LANES] = vz
        table[9 + row, :LANES] = high
        table[12 + row, :LANES] = low
    table[15:17, 2 * LANES :] = 1.0
    for base, shape in (
        (17, wall),
        (20, np.maximum(vy, 0.0) * wall),
        (23, np.maximum(-vy, 0.0) * wall),
    ):
        first, second = pieces(shape, 2)
        table[base, LANES : 2 * LANES] = first
        table[base + 1, LANES : 2 * LANES] = second
        table[base + 2, LANES : 2 * LANES] = first
    return jnp.asarray(table.astype(ml_dtypes.bfloat16))


def own_speed():
    level = lax.axis_index("vel")
    return level, (level.astype(F32) + 0.5) * SPACING - VEL_MAX


def lane_axis(shape, axis):
    return lax.broadcasted_iota(jnp.int32, shape, axis)


def moment_weights():
    row = lane_axis((16, LANES), 0)
    lane = lane_axis((16, LANES), 1)
    vy = ((lane // NV).astype(F32) + 0.5) * SPACING - VEL_MAX
    vz = ((lane % NV).astype(F32) + 0.5) * SPACING - VEL_MAX
    square = vy * vy + vz * vz
    high = square.astype(BF16).astype(F32)
    table = jnp.zeros((16, LANES), F32)
    for at, value in enumerate(
        (1.0, vy, vz, high, square - high, jnp.maximum(-vy, 0.0), jnp.maximum(vy, 0.0))
    ):
        table = jnp.where(row == at, value, table)
    return table.astype(BF16)


def kind_masks(kinds, masks, wx, wy, forward):
    n = wx * wy
    size_y, size_x = kinds.shape
    start_x = lax.axis_index("gx") * wx
    start_y = lax.axis_index("gy") * wy
    behind = jnp.where(forward, 1, -1)
    kind = kinds[...].astype(F32).astype(BF16)
    x = lane_axis((size_x, n), 0)
    own_x = start_x + lane_axis((size_x, n), 1) // wy
    y = lane_axis((size_y, n), 0)
    own_y = start_y + lane_axis((size_y, n), 1) % wy

    def pick(column):
        chosen = jnp.where(x == column, 1.0, 0.0).astype(BF16)
        return jnp.dot(kind, chosen, preferred_element_type=F32)

    def at(table, row):
        return jnp.sum(jnp.where(y == row, table, 0.0), axis=0, keepdims=True)

    here = pick(own_x)
    fluid = 1.0 - at(here, own_y)
    solid_x = at(pick(own_x - behind), own_y)
    solid_b = at(here, own_y - 1)
    solid_a = at(here, own_y + 1)
    column, row = own_x[0:1], own_y[0:1]
    last_x = jnp.logical_and(jnp.logical_not(forward), column == size_x - 1)
    inner_x = jnp.where(last_x, 0.0, fluid)
    inner_b = jnp.where(row == 0, 0.0, fluid)
    inner_a = jnp.where(row == size_y - 1, 0.0, fluid)
    masks[...] = jnp.zeros_like(masks)
    for at_row, value in enumerate(
        (
            fluid,
            inner_x * (1.0 - solid_x),
            inner_x,
            inner_b * (1.0 - solid_b),
            inner_b,
            inner_a * (1.0 - solid_a),
            inner_a,
            fluid * solid_x,
            fluid * solid_b,
            fluid * solid_a,
        )
    ):
        masks[at_row : at_row + 1, :] = value


def moments_kernel(wx, wy, dist, kinds, sums, face_x, face_y, masks, dv, kind, sems):
    n = wx * wy
    copies = {
        first: pltpu.make_async_copy(dist.at[first:last], dv.at[first:last], sems.at[first])
        for first, last in GROUPS
    }
    kind_copy = pltpu.make_async_copy(kinds, kind, sems.at[9])
    kind_copy.start()
    for copy in copies.values():
        copy.start()
    level, vx = own_speed()
    sums[...] = jnp.zeros_like(sums)
    table = moment_weights()
    kind_copy.wait()
    kind_masks(kind, masks, wx, wy, level >= NV // 2)
    forward = level >= NV // 2
    contract = (((1,), (1,)), ((), ()))

    def put(first, step, row):
        for c in range(n // HALF):
            at = first + c * step
            sums[at : at + 1, :] = row[:, c * HALF : (c + 1) * HALF]

    walls_x, walls_y = [None] * 3, [None] * 3
    for k in range(9):
        i, j = divmod(k, 3)
        if k in copies:
            copies[k].wait()
        plane = dv[k]
        high = plane.astype(BF16)
        low = (plane - high.astype(F32)).astype(BF16)
        part = lax.dot_general(table, high, contract, preferred_element_type=F32)
        part = part + lax.dot_general(table, low, contract, preferred_element_type=F32)
        part = part * WEIGHT
        total = part[0:1]
        rows = (
            total,
            vx * total,
            part[1:2],
            part[2:3],
            0.5 * (vx * vx * total + part[3:4] + part[4:5]),
        )
        for f, row in enumerate(rows):
            if k < 8:
                put(f * 32 + k, 8, row)
            else:
                put(TAIL + f * 4, 1, row)
        if i == 0:
            walls_x[j] = total
        if i == 2:
            put(TAIL + (5 + j) * 4, 1, jnp.abs(vx) * jnp.where(forward, total, walls_x[j]))
        if j == 0:
            walls_y[i] = part[5:6] * masks[8:9, :]
        if j == 2:
            put(TAIL + (8 + i) * 4, 1, walls_y[i] + part[6:7] * masks[9:10, :])

    @pl.when(level >= NV // 2)
    def _():
        for j in range(3):
            face_x[j] = dv[6 + j, n - wy : n, :]

    @pl.when(level < NV // 2)
    def _():
        for j in range(3):
            face_x[j] = dv[j, 0:wy, :]

    @pl.when(lax.axis_index("gy") == 0)
    def _():
        for i in range(3):
            for p in range(wx):
                at = p * wy + wy - 1
                face_y[i, p : p + 1, :] = dv[3 * i + 2, at : at + 1, HALF:]

    @pl.when(lax.axis_index("gy") != 0)
    def _():
        for i in range(3):
            for p in range(wx):
                at = p * wy
                face_y[i, p : p + 1, :] = dv[3 * i, at : at + 1, :HALF]


def advect_kernel(wx, wy, dist, table, masks, out, dv, edge_x, edge_y, weights, spread, sems):
    level, vx = own_speed()
    keep = pltpu.make_async_copy(table, weights, sems.at[CHUNKS])
    keep.start()
    row = lane_axis((MASK_ROWS, 7 * HALF), 0)
    column = lane_axis((MASK_ROWS, 7 * HALF), 1)
    select = jnp.where(column // HALF == row, 1.0, 0.0).astype(BF16)
    cx = -TIME_STEP * vx
    face_cx = 6.0 * TIME_STEP * jnp.abs(vx)
    lane = lane_axis((1, HALF), 1)
    q = lane_axis((wy, HALF), 0)

    def speed_y(half):
        return ((lane // NV + half * (NV // 2)).astype(F32) + 0.5) * SPACING - VEL_MAX

    def differences(a):
        four = 4.0 * a[1]
        rest = four - (a[0] + a[2])
        return rest - 2.0 * a[0], a[2] - a[0], 2.0 * a[2] - rest

    def tile(p, half, sign, trace):
        rows = pl.ds(pl.multiple_of(p * wy, wy), wy)
        lanes = slice(half * HALF, (half + 1) * HALF)
        vy = speed_y(half)
        cy = -TIME_STEP * vy
        face_cy = 6.0 * TIME_STEP * jnp.abs(vy)
        d = [[dv[3 * i + j, rows, lanes] for j in range(3)] for i in range(3)]
        fluid, wall_x, own_x, wall_b, own_b, wall_a, own_a = [
            spread[rows, m * HALF : (m + 1) * HALF] for m in range(7)
        ]
        dx = [differences([d[i][j] for i in range(3)]) for j in range(3)]
        for i in range(3):
            dy = differences(d[i])
            for j in range(3):
                value = d[i][j] + fluid * (cx * dx[j][i] + cy * dy[j])
                if i == (0 if sign > 0 else 2):
                    change = own_x * d[i][j]
                    if trace is not None:
                        change = change - wall_x * trace(j, lanes)
                    value = value - face_cx * change
                if half == 1 and j == 0:
                    raw = jnp.where(q == 0, 0.0, pltpu.roll(d[i][2], 1, 0))
                    value = value + face_cy * (wall_b * raw - own_b * d[i][j])
                if half == 0 and j == 2:
                    raw = jnp.where(q == wy - 1, 0.0, pltpu.roll(d[i][0], wy - 1, 0))
                    value = value + face_cy * (wall_a * raw - own_a * d[i][j])
                out[3 * i + j, rows, lanes] = value

    def sweep(sign):
        edge = 0 if sign > 0 else wx - 1
        source = 6 if sign > 0 else 0
        share = wx // CHUNKS
        order = range(CHUNKS) if sign > 0 else range(CHUNKS)[::-1]

        def part(chunk):
            rows = slice(chunk * share * wy, (chunk + 1) * share * wy)
            return pltpu.make_async_copy(dist.at[:, rows], dv.at[:, rows], sems.at[chunk])

        for chunk in order:
            part(chunk).start()
        spread[...] = lax.dot_general(
            masks[...].astype(BF16), select, (((0,), (0,)), ((), ())), preferred_element_type=F32
        )
        edge_x[...] = face_cx * spread[edge * wy : (edge + 1) * wy, HALF : 2 * HALF]
        for chunk in order:
            part(chunk).wait()
            low, high = chunk * share, (chunk + 1) * share
            if chunk == order[0]:
                for half in range(2):
                    tile(edge, half, sign, None)
                low, high = (low + 1, high) if sign > 0 else (low, high - 1)

            @pl.loop(low, high)
            def _(p):
                behind = pl.ds(pl.multiple_of((p - sign) * wy, wy), wy)
                for half in range(2):
                    tile(p, half, sign, lambda j, lanes: dv[source + j, behind, lanes])

    @pl.when(level >= NV // 2)
    def _():
        sweep(1)

    @pl.when(level < NV // 2)
    def _():
        sweep(-1)

    upper = lax.axis_index("gy") != 0

    @pl.when(upper)
    def _():
        for p in range(wx):
            at = p * wy
            edge_y[p : p + 1, :] = spread[at : at + 1, 3 * HALF : 4 * HALF] * (
                6.0 * TIME_STEP * speed_y(1)
            )

    @pl.when(jnp.logical_not(upper))
    def _():
        for p in range(wx):
            at = p * wy + wy - 1
            edge_y[p : p + 1, :] = spread[at : at + 1, 5 * HALF : 6 * HALF] * (
                -6.0 * TIME_STEP * speed_y(0)
            )

    keep.wait()


def edges_kernel(wx, wy, inside, halo_x, inflow, edge_x, out):
    del inside
    level, _ = own_speed()
    forward = level >= NV // 2
    first_x = lax.axis_index("gx") == 0

    def along_x(p, i, outside):
        rows = slice(p * wy, (p + 1) * wy)
        for j in range(3):
            for half in range(2):
                lanes = slice(half * HALF, (half + 1) * HALF)
                out[3 * i + j, rows, lanes] += edge_x[...] * outside(j, lanes)

    @pl.when(forward)
    def _():
        along_x(0, 0, lambda j, at: jnp.where(first_x, inflow[:, at], halo_x[j, :, at]))

    @pl.when(jnp.logical_not(forward))
    def _():
        along_x(wx - 1, 2, lambda j, at: halo_x[j, :, at])


def rows_kernel(wx, wy, inside, rows, halo_y, edge_y, out, fresh, sem):
    del inside
    upper = lax.axis_index("gy") != 0

    def write(row, first, face, half):
        fresh[...] = rows[...]
        for i in range(3):
            for p in range(wx):
                fresh[i, p, row : row + 1, :] += edge_y[p : p + 1, :] * halo_y[i, p : p + 1, :]
        lanes = slice(half * HALF, (half + 1) * HALF)
        copies = [
            pltpu.make_async_copy(
                fresh.at[i], out.at[3 * i + face, :, first : first + 8, lanes], sem.at[i]
            )
            for i in range(3)
        ]
        for copy in copies:
            copy.start()
        for copy in copies:
            copy.wait()

    @pl.when(upper)
    def _():
        write(0, 0, 0, 1)

    @pl.when(jnp.logical_not(upper))
    def _():
        write(7, wy - 8, 2, 0)


def split(value, count):
    out = []
    for _ in range(count):
        piece = value.astype(BF16).astype(F32)
        out.append(piece)
        value = value - piece
    return out


def relax_kernel(
    wx,
    wy,
    sums_a,
    sums_b,
    masks,
    table,
    advected,
    dv,
    out,
    fields_out,
    border,
    coef,
    fields,
    result,
    sems,
):
    n = wx * wy
    level, vx = own_speed()
    is_forward = level >= NV // 2
    parts = range(n // HALF)

    def wide(read, first, step, count):
        return jnp.concatenate(
            [read(slice(first + c * step, first + c * step + count)) for c in parts], axis=1
        )

    def both(rows):
        return sums_a[rows, :] + sums_b[rows, :]

    def slot(rows):
        return jnp.where(lax.axis_index("gx") % 2 == 1, both(rows), sums_b[rows, :])

    fluid = masks[0:1, :]
    coef[...] = jnp.zeros_like(coef)
    log2e = math.log2(math.e)

    def store(planes, start, value, count):
        for piece_at, piece in enumerate(split(value, count)):
            coef[planes, start + piece_at, :] = piece

    for planes, where, s in (
        (slice(0, 8), 0, [wide(both, f * 32, 8, 8) for f in range(5)]),
        (slice(8, 9), 8, [wide(both, TAIL + f * 4, 1, 1) for f in range(5)]),
    ):
        rho = s[0]
        ux, uy, uz = s[1] / rho, s[2] / rho, s[3] / rho
        temp = 2.0 / 3.0 * (s[4] / rho - 0.5 * (ux * ux + uy * uy + uz * uz))
        for f, value in enumerate((rho, ux, uy, uz, temp)):
            at = f * 9 + where
            fields[at : at + value.shape[0], :] = value
        rate = rho * jnp.sqrt(temp) / RAREFACTION * TIME_STEP * fluid
        slope = (0.5 * log2e) / temp
        height = (
            2.0 * jnp.log2(rho)
            - jnp.log2(temp)
            + math.log2(TIME_STEP / RAREFACTION)
            - slope * ((vx - ux) * (vx - ux) + uy * uy + uz * uz)
        )
        height = jnp.where(fluid == 0.0, -1e30, height)
        store(planes, 0, height, 3)
        store(planes, 3, 2.0 * slope * uy, 3)
        store(planes, 6, 2.0 * slope * uz, 3)
        store(planes, 9, -slope, 3)
        store(planes, 12, -slope, 3)
        store(planes, 15, rate, 2)

    def store_wall(k, start, value):
        first, second = split(value, 2)
        coef[k, start : start + 1, :] = first
        coef[k, start + 1 : start + 2, :] = first
        coef[k, start + 2 : start + 3, :] = second

    scale = 6.0 * TIME_STEP / wall_scale()
    forward = is_forward.astype(F32)
    gauss_x = jnp.exp(jnp.full((1, n), -0.5, F32) * (vx * vx)) * scale
    solid_x = masks[7:8, :] * gauss_x * jnp.abs(vx)
    solid_b = masks[8:9, :] * gauss_x
    solid_a = masks[9:10, :] * gauss_x
    for j in range(3):
        value = solid_x * wide(slot, TAIL + (5 + j) * 4, 1, 1)
        store_wall(j, 17, value * forward)
        store_wall(6 + j, 17, value * (1.0 - forward))
    for i in range(3):
        value = wide(both, TAIL + (8 + i) * 4, 1, 1)
        store_wall(3 * i, 20, solid_b * value)
        store_wall(3 * i + 2, 23, solid_a * value)

    weights = table[...]
    chunk = 128
    block = 2 * chunk
    copies = []
    for k in range(9):
        for start in range(0, n, chunk):
            rows = slice(start, start + chunk)
            spread = lax.dot_general(
                coef[k, :, rows].astype(BF16),
                weights,
                (((0,), (0,)), ((), ())),
                preferred_element_type=F32,
            )
            rate = spread[:, 2 * LANES :]
            for half in range(2):
                lanes = slice(half * HALF, (half + 1) * HALF)
                target = jnp.exp2(spread[:, lanes])
                wall = spread[:, LANES + half * HALF : LANES + (half + 1) * HALF]
                result[k, rows, lanes] = (
                    advected[k, rows, lanes] - rate * dv[k, rows, lanes] + (target + wall)
                )
            if (start + chunk) % block == 0:
                done = slice(start + chunk - block, start + chunk)
                copy = pltpu.make_async_copy(
                    result.at[k, done], out.at[k, done], sems.at[len(copies)]
                )
                copy.start()
                copies.append(copy)
    upper = lax.axis_index("gy") != 0

    def keep(first, face, half):
        for i in range(3):
            for p in range(wx):
                at = slice(p * wy + first, p * wy + first + 8)
                border[i, p] = result[3 * i + face, at, half * HALF : (half + 1) * HALF]

    @pl.when(upper)
    def _():
        keep(0, 0, 1)

    @pl.when(jnp.logical_not(upper))
    def _():
        keep(wy - 8, 2, 0)

    for p in range(wx):
        fields_out[:, p, :] = fields[0:45, p * wy : (p + 1) * wy]
    for copy in copies:
        copy.wait()


def exchanges():
    count, columns = lax.axis_size("vel"), lax.axis_size("gx")
    return tuple(
        [
            (v * columns + g, (v ^ steps[g % 2]) * columns + g)
            for v in range(count)
            for g in range(columns)
        ]
        for steps in zip(*ORDERS)
    )


def upwind_pairs():
    count = lax.axis_size("gx")
    pairs = []
    for v in range(lax.axis_size("vel")):
        step = 1 if v >= NV // 2 else -1
        for g in range(count):
            if 0 <= g + step < count:
                pairs.append((v * count + g, v * count + g + step))
    return pairs


def vmem(shape):
    return pltpu.VMEM(shape, F32)


def in_vmem(x):
    return pltpu.with_memory_space_constraint(x, pltpu.VMEM)


def shards(dist, cell_kind, inflow):
    wx, wy = dist.shape[2], dist.shape[3]
    n = wx * wy
    whole = pl.BlockSpec(memory_space=pltpu.VMEM)
    anywhere = pl.BlockSpec(memory_space=pl.ANY)
    planes = pltpu.with_memory_space_constraint(dist.reshape(9, n, LANES), pltpu.HBM)
    sums, face_x, face_y, masks = pl.pallas_call(
        lambda *refs: moments_kernel(wx, wy, *refs),
        out_shape=(
            vmem((SUM_ROWS, HALF)),
            vmem((3, wy, LANES)),
            vmem((3, wx, HALF)),
            vmem((MASK_ROWS, n)),
        ),
        in_specs=[anywhere, anywhere],
        out_specs=(whole, whole, whole, whole),
        scratch_shapes=[
            pltpu.VMEM((9, n, LANES), F32),
            pltpu.VMEM(cell_kind.shape[::-1], jnp.int32),
            pltpu.SemaphoreType.DMA((10,)),
        ],
        compiler_params=pltpu.CompilerParams(vmem_limit_bytes=16 << 20),
        cost_estimate=pl.CostEstimate(
            flops=2 * 32 * 9 * n * LANES, bytes_accessed=4 * 9 * n * LANES, transcendentals=0
        ),
        name="moments",
    )(planes, pltpu.with_memory_space_constraint(cell_kind.T, pltpu.HBM))
    table = spread_weights()
    advected, held, edge_x, edge_y, table = pl.pallas_call(
        lambda *refs: advect_kernel(wx, wy, *refs),
        out_shape=(
            vmem((9, n, LANES)),
            vmem((9, n, LANES)),
            vmem((wy, HALF)),
            vmem((wx, HALF)),
            pltpu.VMEM(table.shape, table.dtype),
        ),
        in_specs=[anywhere, anywhere, whole],
        out_specs=(whole,) * 5,
        scratch_shapes=[pltpu.VMEM((n, 7 * HALF), F32), pltpu.SemaphoreType.DMA((CHUNKS + 1,))],
        compiler_params=pltpu.CompilerParams(vmem_limit_bytes=8 << 20),
        cost_estimate=pl.CostEstimate(
            flops=20 * 9 * n * LANES, bytes_accessed=12 * 9 * n * LANES, transcendentals=0
        ),
        name="advect",
    )(planes, pltpu.with_memory_space_constraint(table, pltpu.HBM), masks)
    steps = exchanges()
    def partner(value, pairs):
        return lax.ppermute(value, ("vel", "gx"), pairs)

    odd = lax.axis_index("gx") % 2 == 1
    row = jnp.arange(SUM_ROWS, dtype=jnp.int32)[:, None]
    swapped = jnp.logical_and(odd, jnp.logical_and(row >= SLOT.start, row < SLOT.stop))
    total = sums + partner(sums, steps[0])
    total = jnp.where(swapped, 0.0, total) + partner(total, steps[1])
    halo_x = lax.ppermute(face_x, ("vel", "gx"), upwind_pairs())
    total, halo_x, edge_x, edge_y = lax.optimization_barrier((total, halo_x, edge_x, edge_y))
    total = total + partner(total, steps[2])
    advected = pl.pallas_call(
        lambda *refs: edges_kernel(wx, wy, *refs),
        out_shape=vmem((9, n, LANES)),
        in_specs=[whole] * 4,
        out_specs=whole,
        input_output_aliases={0: 0},
        compiler_params=pltpu.CompilerParams(vmem_limit_bytes=4 << 20),
        name="edges",
    )(in_vmem(advected), halo_x, inflow[None, :], edge_x)
    other = partner(total, steps[3])
    halo_y = lax.ppermute(face_y, "gy", [(0, 1), (1, 0)])
    fresh, fields, border = pl.pallas_call(
        lambda *refs: relax_kernel(wx, wy, *refs),
        out_shape=(
            jax.ShapeDtypeStruct((9, n, LANES), F32),
            jax.ShapeDtypeStruct((45, wx, wy), F32),
            vmem((3, wx, 8, HALF)),
        ),
        in_specs=[whole] * 6,
        out_specs=(anywhere, whole, whole),
        scratch_shapes=[
            pltpu.VMEM((9, COEF_ROWS, n), F32),
            pltpu.VMEM((48, n), F32),
            pltpu.VMEM((9, n, LANES), F32),
            pltpu.SemaphoreType.DMA((9 * n // 256,)),
        ],
        compiler_params=pltpu.CompilerParams(vmem_limit_bytes=16 << 20),
        name="relax",
    )(total, other, masks, table, in_vmem(advected), in_vmem(held))
    fresh = pl.pallas_call(
        lambda *refs: rows_kernel(wx, wy, *refs),
        out_shape=jax.ShapeDtypeStruct((9, wx, wy, LANES), F32),
        in_specs=[anywhere, whole, whole, whole],
        out_specs=anywhere,
        scratch_shapes=[pltpu.VMEM((3, wx, 8, HALF), F32), pltpu.SemaphoreType.DMA((3,))],
        input_output_aliases={0: 0},
        compiler_params=pltpu.CompilerParams(vmem_limit_bytes=4 << 20),
        name="rows",
    )(fresh.reshape(9, wx, wy, LANES), border, halo_y, edge_y)
    return (fresh.reshape(dist.shape), fields.reshape(5, 3, 3, wx, wy))


def solution(mesh):
    in_specs = (P(None, None, "gx", "gy", "vel"), P(), P("vel"))
    out_specs = (P(None, None, "gx", "gy", "vel"), P(None, None, None, "gx", "gy"))
    return jax.shard_map(shards, mesh=mesh, in_specs=in_specs, out_specs=out_specs, check_vma=False)
```
